1024 devices in a mesh: dp: 32 (over x, y_lo, core), tensor: 32 (over z, y_hi).
Axes of the slice: x: 8, y: 8 (y_hi: 4, y_lo: 2; y = y_hi * 2 + y_lo), z: 8, core: 2. Of those that a mesh axis runs over, the one named last changes fastest.
Arguments:
- activations: bfloat16 [4096, 8192], P('dp', 'tensor'), may hold values from -56 to 56
- w_query: bfloat16 [8192, 8192], P(None, 'tensor'), may hold values from -0.0625 to 0.0625
- w_keyval: bfloat16 [8192, 2048], P(None, 'tensor'), may hold values from -0.0625 to 0.0625
- w_out: bfloat16 [8192, 8192], P('tensor'), may hold values from -0.0625 to 0.0625
- targets: int32 [1024], replicated, may hold values from 0 to 2047, as said below
- segments: int32 [5120], P('dp'), may hold values from -64 to 100003, as said below
Outputs:
- mixed: bfloat16 [5120, 8192], P('dp', 'tensor')
The draws below stay inside these ranges and needn't reach their ends.
Inputs may be any that keep to these rules, and one draw needn't show every extreme that they name: All entries differ. targets // 64 is a destination block, never the source block s of entry s * 32 + m, and targets % 64 is a slot below 64; each source's tail is a run of four documents, each going whole to its own destination and landing in consecutive slots in order; every slot of some destination blocks, the last block among them, is used. In every block the arriving documents fill slots from 0 without gaps. `segments`: labels of the first 96 rows of a block are small positive numbers, those of arriving documents 100000 and up, and every unused arriving slot t carries -(t + 1); labels match the documents that targets places.
All inputs are finite; a program needn't handle non-finite values.
Results may differ from the reference program's by a relative error of at most 0.02.
Values may be sent and summed in bfloat16 or wider, within the bound.
No kernel may reach another device: no remote copies, remote signals or barrier semaphores. Data moves between devices by JAX's collectives and lax.ppermute only.
A program may use at most 32 MiB of HBM per device.

```python
import math
import jax
import jax.numpy as jnp
from jax import lax

D = 8192
HQ = 64
KVH = 8
HD = 128
SEQ_DEV = 128
MOVE = 32
KEEP = 96
RECV = 64
ROWS_BAL = 160
TOKENS = 4096
N_DP = 32
N_TENSOR = 32


def plan_moves(key):
    half = MOVE // 2
    key_order = jax.random.fold_in(key, 101)
    key_first = jax.random.fold_in(key, 102)
    key_second = jax.random.fold_in(key, 103)
    shuffled = jax.random.permutation(key_order, N_DP).astype(jnp.int32)
    places = jnp.arange(N_DP)
    full_place = N_DP % 4
    last_at = jnp.argmax(shuffled == N_DP - 1)
    order = shuffled.at[last_at].set(shuffled[full_place]).at[full_place].set(N_DP - 1)
    first_cut = jax.random.randint(key_first, (N_DP,), 1, half - 1)
    spread = jax.random.randint(key_second, (N_DP,), 0, 1 << 20)
    second_cut = first_cut + 1 + spread % (half - 1 - first_cut)
    shorts = jnp.stack([first_cut, second_cut - first_cut, half - second_cut], axis=1)
    column = jnp.arange(4)[None, :]
    long_at = ((N_DP - 1 - places) % 4)[:, None]
    short_pick = jnp.clip(jnp.where(column < long_at, column, column - 1), 0, 2)
    lengths = jnp.where(column == long_at, half, jnp.take_along_axis(shorts, short_pick, axis=1))
    from_place = (places[:, None] - 1 - column) % N_DP
    got_length = lengths[from_place, column]
    got_offset = jnp.cumsum(got_length, axis=1) - got_length
    return (order, lengths, got_length, got_offset)


def draw_activations(key, part):
    key = jax.random.fold_in(key, 11)
    key_noise = jax.random.fold_in(key, 1)
    values = jnp.clip(jax.random.normal(key_noise, (TOKENS, D), jnp.float32), -6.0, 6.0)
    return values.astype(jnp.bfloat16)


def draw_targets(key, part):
    order, lengths, got_length, got_offset = plan_moves(key)
    places = jnp.arange(N_DP)
    starts = jnp.cumsum(lengths, axis=1) - lengths
    inside = jnp.arange(MOVE)
    doc_index = jnp.sum(inside[None, :, None] >= starts[:, None, 1:], axis=2)
    within = inside[None, :] - jnp.take_along_axis(starts, doc_index, axis=1)
    dest_place = (places[:, None] + 1 + doc_index) % N_DP
    value = order[dest_place] * RECV + got_offset[dest_place, doc_index] + within
    by_source = jnp.zeros((N_DP, MOVE), jnp.int32).at[order].set(value.astype(jnp.int32))
    return by_source.reshape(-1).astype(jnp.int32)


def draw_segments(key, part):
    order, lengths, got_length, got_offset = plan_moves(key)
    key = jax.random.fold_in(key, 7)
    start_flag = jax.random.randint(key, (N_DP, KEEP), 0, 32) == 0
    start_flag = start_flag.at[:, 0].set(True)
    kept_label = jnp.cumsum(start_flag.astype(jnp.int32), axis=1)
    slots = jnp.arange(RECV)
    doc_of_slot = jnp.sum(slots[None, :, None] >= got_offset[:, None, 1:], axis=2)
    filled = slots[None, :] < jnp.sum(got_length, axis=1)[:, None]
    recv_label = jnp.where(filled, 100000 + doc_of_slot, -(slots[None, :] + 1))
    by_dest = jnp.zeros((N_DP, RECV), jnp.int32).at[order].set(recv_label.astype(jnp.int32))
    return jnp.concatenate([kept_label, by_dest], axis=1).reshape(-1).astype(jnp.int32)


def level_of(stream_key, shape, cuts, smallest, high):
    def one(position, blocks):
        draws = jax.random.uniform(jax.random.fold_in(jax.random.fold_in(stream_key, 6), position), (blocks,), jnp.float32, smallest / len(cuts), high / len(cuts))
        return jnp.repeat(jnp.exp(draws), shape[position] // blocks).reshape((-1,) + (1,) * (len(shape) - position - 1))

    factor_of = one(*cuts[0])
    for cut in cuts[1:]:
        factor_of = factor_of * one(*cut)
    return factor_of


def scatter_about(key, extent, scale, limit, cuts=(), held_as=jnp.bfloat16):
    loudness = level_of(key, extent, cuts, -0.22, 0.18) if cuts else 1.0
    values = jax.random.normal(key, extent, jnp.float32) * scale * loudness
    return jnp.minimum(jnp.maximum(values, -limit), limit).astype(held_as)


def setup_inputs(seed: int = 0) -> dict:
    arg_keys = jax.random.split(jax.random.key(seed), 7)
    activations = draw_activations(jax.random.fold_in(arg_keys[6], 71), 0)
    w_query = scatter_about(arg_keys[1], (D, HQ * HD), D ** -0.5, 0.0625, ((1, 32),))
    w_keyval = scatter_about(arg_keys[2], (D, 2 * KVH * HD), D ** -0.5, 0.0625, ((1, 32),))
    w_out = scatter_about(arg_keys[3], (HQ * HD, D), (HQ * HD) ** -0.5, 0.0625, ((0, 32),))
    targets = draw_targets(jax.random.fold_in(arg_keys[6], 71), 0)
    segments = draw_segments(jax.random.fold_in(arg_keys[6], 71), 0)
    return dict(activations=activations, w_query=w_query, w_keyval=w_keyval, w_out=w_out, targets=targets, segments=segments)


rope_base = 500000.0

def rotation_tables(positions):
    half = HD // 2
    freqs = rope_base ** (-(jnp.arange(half, dtype=jnp.float32) * 2.0 / HD))
    angles = positions.astype(jnp.float32)[:, None] * freqs[None, :]
    return (jnp.cos(angles), jnp.sin(angles))

def rotate(values, cosine, sine):
    half = HD // 2
    first = values[..., :half]
    second = values[..., half:]
    cosine = cosine[:, None, :]
    sine = sine[:, None, :]
    return jnp.concatenate([first * cosine - second * sine, second * cosine + first * sine], axis=-1)

def doc_layout(segment):
    same = segment[:, None] == segment[None, :]
    indices = jnp.arange(segment.shape[0])
    earlier = indices[None, :] < indices[:, None]
    positions = lax.optimization_barrier(jnp.sum(jnp.logical_and(same, earlier), axis=1)).astype(jnp.int32)
    visible = jnp.logical_and(same, indices[None, :] <= indices[:, None])
    return (positions, visible)

def attend(query_rot, key_rot, value_rows, visible):
    count = query_rot.shape[0]
    scores = jnp.einsum('rkgd,ckd->kgrc', query_rot.astype(jnp.float32), key_rot.astype(jnp.float32)) / math.sqrt(HD)
    scores = jnp.where(visible[None, None], scores, -1e+30)
    top = lax.optimization_barrier(jnp.max(scores, axis=-1, keepdims=True))
    expd = jnp.exp(scores - top)
    weights = (expd / lax.optimization_barrier(jnp.sum(expd, axis=-1, keepdims=True))).astype(jnp.bfloat16)
    result = jnp.einsum('kgrc,ckd->rkgd', weights.astype(jnp.float32), value_rows.astype(jnp.float32))
    return result.astype(jnp.bfloat16).reshape(count, -1)

def reference(activations, w_query, w_keyval, w_out, targets, segments):
    blocks = activations.reshape(N_DP, SEQ_DEV, D)
    tails = blocks[:, KEEP:].reshape(N_DP * MOVE, D)
    arrived = jnp.zeros((N_DP * RECV, D), jnp.bfloat16).at[targets].set(tails)
    balanced = jnp.concatenate([blocks[:, :KEEP], arrived.reshape(N_DP, RECV, D)], axis=1)
    labels = segments.reshape(N_DP, ROWS_BAL)
    share = HQ * HD // N_TENSOR
    out_wide = w_out.astype(jnp.float32).reshape(N_TENSOR, share, D)
    group = HQ // KVH

    def one_block(pair):
        rows_in, segment = pair
        positions, visible = doc_layout(segment)
        cosine, sine = rotation_tables(positions)
        query = jnp.dot(rows_in, w_query, preferred_element_type=jnp.float32).reshape(ROWS_BAL, HQ, HD)
        query = rotate(query, cosine, sine).astype(jnp.bfloat16).reshape(ROWS_BAL, KVH, group, HD)
        keyval = jnp.dot(rows_in, w_keyval, preferred_element_type=jnp.float32).astype(jnp.bfloat16)
        key_raw = keyval[:, :KVH * HD].reshape(ROWS_BAL, KVH, HD)
        value_rows = keyval[:, KVH * HD:].reshape(ROWS_BAL, KVH, HD)
        key_rot = rotate(key_raw.astype(jnp.float32), cosine, sine).astype(jnp.bfloat16)
        attended = attend(query, key_rot, value_rows, visible)
        pieces = attended.astype(jnp.float32).reshape(ROWS_BAL, N_TENSOR, share)
        partial_terms = jnp.einsum('rnc,ncd->nrd', pieces, out_wide).astype(jnp.bfloat16)
        partial_terms = lax.optimization_barrier(partial_terms)
        return lax.optimization_barrier(jnp.sum(partial_terms.astype(jnp.float32), axis=0)).astype(jnp.bfloat16)
    mixed = lax.map(one_block, (balanced, labels))
    return mixed.reshape(N_DP * ROWS_BAL, D)
```

```python
import math

import jax
import jax.numpy as jnp
from jax import lax
from jax.sharding import Mesh
from jax.sharding import PartitionSpec as P

HQ = 64
KVH = 8
HD = 128
KEEP = 96
MOVE = 32
RECV = 64
SEQ = 128

N_Z = 8
N_Y = 4
DP = ("x", "yl", "core")
TENSOR = ("z", "yh")

rope_base = 500000.0


def rotation_tables(positions):
    half = HD // 2
    freqs = rope_base ** (-(jnp.arange(half, dtype=jnp.float32) * 2.0 / HD))
    angles = positions.astype(jnp.float32)[:, None] * freqs[None, :]
    return (jnp.cos(angles), jnp.sin(angles))


def rotate(values, cosine, sine):
    half = HD // 2
    first = values[..., :half]
    second = values[..., half:]
    cosine = cosine[:, None, :]
    sine = sine[:, None, :]
    return jnp.concatenate(
        [first * cosine - second * sine, second * cosine + first * sine], axis=-1
    )


def doc_layout(segment):
    same = segment[:, None] == segment[None, :]
    indices = jnp.arange(segment.shape[0])
    earlier = indices[None, :] < indices[:, None]
    positions = jnp.sum(jnp.logical_and(same, earlier), axis=1)
    visible = jnp.logical_and(same, indices[None, :] <= indices[:, None])
    return (positions, visible)


def attend(query_rot, key_rot, value_rows, visible):
    count = query_rot.shape[0]
    scores = jnp.einsum(
        "rkgd,ckd->kgrc", query_rot, key_rot, preferred_element_type=jnp.float32
    ) / math.sqrt(HD)
    scores = jnp.where(visible[None, None], scores, -1e30)
    top = jnp.max(scores, axis=-1, keepdims=True)
    expd = jnp.exp(scores - top)
    weights = (expd / jnp.sum(expd, axis=-1, keepdims=True)).astype(jnp.bfloat16)
    result = jnp.einsum("kgrc,ckd->rkgd", weights, value_rows, preferred_element_type=jnp.float32)
    return result.astype(jnp.bfloat16).reshape(count, -1)


def keyval_routes():
    half = N_Z * N_Y // 2
    return [(s, N_Y * ((s % half) // 2) + (s % 2) + 2 * (s // half)) for s in range(2 * half)]


def sum_over_y(rows):
    me = lax.axis_index("yh")
    width = rows.shape[1] // N_Y
    total = lax.dynamic_slice_in_dim(rows, me * width, width, 1).astype(jnp.float32)
    for k in range(1, N_Y):
        piece = lax.dynamic_slice_in_dim(rows, lax.rem(me + k, N_Y) * width, width, 1)
        piece = lax.ppermute(piece, "yh", [(i, (i + k) % N_Y) for i in range(N_Y)])
        total = total + piece.astype(jnp.float32)
    return total.astype(jnp.bfloat16)


def shards(activations, w_query, w_keyval, w_out, targets, segments):
    block = lax.axis_index(DP)
    tail_docs = lax.dynamic_slice_in_dim(targets, block * MOVE, MOVE) // RECV
    labels = jnp.concatenate([segments[:KEEP], -1 - tail_docs])
    positions, visible = doc_layout(labels)
    cosine, sine = rotation_tables(positions)

    piece = lax.all_gather(activations, "yh", axis=1, tiled=True)
    piece = lax.all_gather(piece, "z", axis=1, tiled=True)
    query = jnp.dot(piece, w_query, preferred_element_type=jnp.float32)
    keyval = jnp.dot(piece, w_keyval, preferred_element_type=jnp.float32).astype(jnp.bfloat16)
    keyval = lax.ppermute(keyval, TENSOR, keyval_routes())
    keyval = lax.all_gather(keyval, "yh", axis=1, tiled=True)
    key = keyval[:, :HD].reshape(SEQ, 1, HD)
    value = keyval[:, HD:].reshape(SEQ, 1, HD)
    query_rot = rotate(query.reshape(SEQ, 2, HD), cosine, sine).astype(jnp.bfloat16)
    key_rot = rotate(key.astype(jnp.float32), cosine, sine).astype(jnp.bfloat16)
    attended = attend(query_rot.reshape(SEQ, 1, 2, HD), key_rot, value, visible)

    partial = lax.dot_general(
        w_out, attended, (((0,), (1,)), ((), ())), preferred_element_type=jnp.float32
    ).astype(jnp.bfloat16)
    summed = lax.psum_scatter(partial, "z", scatter_dimension=0, tiled=True)
    mixed = sum_over_y(summed.T)

    slots = lax.iota(jnp.int32, RECV)
    wanted = targets - block * RECV
    select = (slots[:, None] == wanted[None, :]).astype(jnp.bfloat16)
    tails = lax.all_gather(mixed[KEEP:], DP, axis=0, tiled=True)
    arrived = jnp.dot(select, tails, preferred_element_type=jnp.float32).astype(jnp.bfloat16)
    return jnp.concatenate([mixed[:KEEP], arrived], axis=0)


def solution(mesh):
    fine = Mesh(
        mesh.devices.reshape(8, 2, 2, N_Z, N_Y), ("x", "yl", "core", "z", "yh")
    )
    placed = (
        P(DP, TENSOR),
        P(None, TENSOR),
        P(None, TENSOR),
        P(TENSOR, None),
        P(),
        P(DP),
    )
    return jax.shard_map(
        shards, mesh=fine, in_specs=placed, out_specs=P(DP, TENSOR), check_vma=False
    )
```

```python
import math

import jax
import jax.numpy as jnp
from jax import lax
from jax.sharding import Mesh
from jax.sharding import PartitionSpec as P

HQ = 64
KVH = 8
HD = 128
KEEP = 96
MOVE = 32
RECV = 64
SEQ = 128

N_Z = 8
N_Y = 4
DP = ("x", "yl", "core")
TENSOR = ("z", "yh")

rope_base = 500000.0


def rotation_tables(positions):
    half = HD // 2
    freqs = rope_base ** (-(jnp.arange(half, dtype=jnp.float32) * 2.0 / HD))
    angles = positions.astype(jnp.float32)[:, None] * freqs[None, :]
    return (jnp.cos(angles), jnp.sin(angles))


def rotate(values, cosine, sine):
    half = HD // 2
    first = values[..., :half]
    second = values[..., half:]
    cosine = cosine[:, None, :]
    sine = sine[:, None, :]
    return jnp.concatenate(
        [first * cosine - second * sine, second * cosine + first * sine], axis=-1
    )


def doc_layout(segment):
    same = segment[:, None] == segment[None, :]
    indices = jnp.arange(segment.shape[0])
    earlier = indices[None, :] < indices[:, None]
    positions = jnp.sum(jnp.logical_and(same, earlier), axis=1)
    visible = jnp.logical_and(same, indices[None, :] <= indices[:, None])
    return (positions, visible)


def attend(query_rot, key_rot, value_rows, visible):
    count = query_rot.shape[0]
    scores = jnp.einsum(
        "rkgd,ckd->kgrc", query_rot, key_rot, preferred_element_type=jnp.float32
    ) / math.sqrt(HD)
    scores = jnp.where(visible[None, None], scores, -1e30)
    top = jnp.max(scores, axis=-1, keepdims=True)
    expd = jnp.exp(scores - top)
    weights = (expd / jnp.sum(expd, axis=-1, keepdims=True)).astype(jnp.bfloat16)
    result = jnp.einsum("kgrc,ckd->rkgd", weights, value_rows, preferred_element_type=jnp.float32)
    return result.astype(jnp.bfloat16).reshape(count, -1)


def ring(n, k):
    return [(i, (i + k) % n) for i in range(n)]


def keyval_routes(k):
    half = N_Z * N_Y // 2
    return [
        (s, N_Y * ((s % half) // 2) + (s % 2 + 2 * (s // half) + k) % N_Y) for s in range(2 * half)
    ]


def gather_y(rows):
    me = lax.axis_index("yh")
    pieces = [rows] + [lax.ppermute(rows, "yh", ring(N_Y, k)) for k in range(1, N_Y)]
    stack = jnp.stack(pieces)
    return jnp.concatenate(
        [lax.dynamic_index_in_dim(stack, (me - j) % N_Y, 0, False) for j in range(N_Y)], axis=1
    )


def sum_pieces(pieces):
    return jnp.sum(pieces.astype(jnp.float32), axis=0).astype(jnp.bfloat16)


def scatter_sum(attended, w_out):
    n = N_Z * N_Y
    partial = jnp.einsum(
        "rk,kdn->drn",
        attended,
        w_out.reshape(w_out.shape[0], n, -1),
        preferred_element_type=jnp.float32,
    ).astype(jnp.bfloat16)
    return sum_pieces(lax.all_to_all(partial, TENSOR, 0, 0, tiled=True))


def sum_over_y(rows):
    me = lax.axis_index("yh")
    width = rows.shape[1] // N_Y
    total = lax.dynamic_slice_in_dim(rows, me * width, width, 1).astype(jnp.float32)
    for k in range(1, N_Y):
        piece = lax.dynamic_slice_in_dim(rows, lax.rem(me + k, N_Y) * width, width, 1)
        piece = lax.ppermute(piece, "yh", [(i, (i + k) % N_Y) for i in range(N_Y)])
        total = total + piece.astype(jnp.float32)
    return total.astype(jnp.bfloat16)


def shards(activations, w_query, w_keyval, w_out, targets, segments):
    block = lax.axis_index(DP)
    tail_docs = lax.dynamic_slice_in_dim(targets, block * MOVE, MOVE) // RECV
    labels = jnp.concatenate([segments[:KEEP], -1 - tail_docs])
    positions, visible = doc_layout(labels)
    cosine, sine = rotation_tables(positions)

    z_me = lax.axis_index("z")
    y_me = lax.axis_index("yh")
    own = gather_y(activations)
    depth = own.shape[1]

    def times(weight, chunk, k):
        rows = lax.dynamic_slice_in_dim(weight, ((z_me + k) % N_Z) * depth, depth, 0)
        return jnp.dot(chunk, rows, preferred_element_type=jnp.float32)

    query = times(w_query, own, 0)
    keyval = times(w_keyval, own, 0)
    up, down = own, own
    for step in range(1, N_Z // 2):
        up = lax.ppermute(up, "z", ring(N_Z, 1))
        down = lax.ppermute(down, "z", ring(N_Z, -1))
        query = query + times(w_query, up, -step) + times(w_query, down, step)
        keyval = keyval + times(w_keyval, up, -step) + times(w_keyval, down, step)
    half = SEQ // 2
    up = lax.ppermute(up[:half], "z", ring(N_Z, 1))
    down = lax.ppermute(down[half:], "z", ring(N_Z, -1))
    last = jnp.concatenate([up, down], axis=0)
    keyval = (keyval + times(w_keyval, last, N_Z // 2)).astype(jnp.bfloat16)
    pieces = [lax.ppermute(keyval, TENSOR, keyval_routes(k)) for k in range(N_Y)]
    query = query + times(w_query, last, N_Z // 2)

    stack = jnp.stack(pieces)
    roles = [lax.dynamic_index_in_dim(stack, (y_me - r) % N_Y, 0, False) for r in range(N_Y)]
    key = jnp.concatenate(roles[:2], axis=1).reshape(SEQ, 1, HD)
    value = jnp.concatenate(roles[2:], axis=1).reshape(SEQ, 1, HD)
    query_rot = rotate(query.reshape(SEQ, 2, HD), cosine, sine).astype(jnp.bfloat16)
    key_rot = rotate(key.astype(jnp.float32), cosine, sine).astype(jnp.bfloat16)
    attended = attend(query_rot.reshape(SEQ, 1, 2, HD), key_rot, value, visible)

    partial = lax.dot_general(
        w_out, attended[:KEEP], (((0,), (1,)), ((), ())), preferred_element_type=jnp.float32
    ).astype(jnp.bfloat16)
    kept = lax.psum_scatter(partial, "z", scatter_dimension=0, tiled=True)
    moving = scatter_sum(attended[KEEP:], w_out)
    kept = sum_over_y(kept.T)

    slots = lax.iota(jnp.int32, RECV)
    wanted = targets - block * RECV
    select = (slots[:, None] == wanted[None, :]).astype(jnp.bfloat16)
    tails = jnp.broadcast_to(moving[None], (targets.shape[0] // MOVE,) + moving.shape)
    tails = lax.all_to_all(tails, DP, 0, 0, tiled=True).reshape(targets.shape[0], -1)
    arrived = jnp.dot(select, tails, preferred_element_type=jnp.float32).astype(jnp.bfloat16)
    return jnp.concatenate([kept, arrived], axis=0)


def solution(mesh):
    fine = Mesh(
        mesh.devices.reshape(8, 2, 2, N_Z, N_Y), ("x", "yl", "core", "z", "yh")
    )
    placed = (
        P(DP, TENSOR),
        P(None, TENSOR),
        P(None, TENSOR),
        P(TENSOR, None),
        P(),
        P(DP),
    )
    return jax.shard_map(
        shards, mesh=fine, in_specs=placed, out_specs=P(DP, TENSOR), check_vma=False
    )
```

```python
import math

import jax
import jax.numpy as jnp
from jax import lax
from jax.sharding import Mesh
from jax.sharding import PartitionSpec as P

HQ = 64
KVH = 8
HD = 128
KEEP = 96
MOVE = 32
RECV = 64

N_Z = 8
N_Y = 4
DP = ("x", "yl", "core")
TENSOR = ("z", "yh")

rope_base = 500000.0


def rotation_tables(positions):
    half = HD // 2
    freqs = rope_base ** (-(jnp.arange(half, dtype=jnp.float32) * 2.0 / HD))
    angles = positions.astype(jnp.float32)[:, None] * freqs[None, :]
    return (jnp.cos(angles), jnp.sin(angles))


def rotate(values, cosine, sine):
    half = HD // 2
    first = values[..., :half]
    second = values[..., half:]
    cosine = cosine[:, None, :]
    sine = sine[:, None, :]
    return jnp.concatenate(
        [first * cosine - second * sine, second * cosine + first * sine], axis=-1
    )


def doc_layout(segment):
    same = segment[:, None] == segment[None, :]
    indices = jnp.arange(segment.shape[0])
    earlier = indices[None, :] < indices[:, None]
    positions = jnp.sum(jnp.logical_and(same, earlier), axis=1)
    visible = jnp.logical_and(same, indices[None, :] <= indices[:, None])
    return (positions, visible)


def attend(query_rot, key_rot, value_rows, visible):
    count = query_rot.shape[0]
    scores = jnp.einsum(
        "rkgd,ckd->kgrc", query_rot, key_rot, preferred_element_type=jnp.float32
    ) / math.sqrt(HD)
    scores = jnp.where(visible[None, None], scores, -1e30)
    top = jnp.max(scores, axis=-1, keepdims=True)
    expd = jnp.exp(scores - top)
    weights = (expd / jnp.sum(expd, axis=-1, keepdims=True)).astype(jnp.bfloat16)
    result = jnp.einsum("kgrc,ckd->rkgd", weights, value_rows, preferred_element_type=jnp.float32)
    return result.astype(jnp.bfloat16).reshape(count, -1)


def ring(n, k):
    return [(i, (i + k) % n) for i in range(n)]


def keyval_routes(k):
    half = N_Z * N_Y // 2
    return [
        (s, N_Y * ((s % half) // 2) + (s % 2 + 2 * (s // half) + k) % N_Y) for s in range(2 * half)
    ]


def sum_pieces(pieces):
    return jnp.sum(pieces.astype(jnp.float32), axis=0).astype(jnp.bfloat16)


def scatter_sum(attended, w_out):
    n = N_Z * N_Y
    partial = jnp.einsum(
        "rk,kdn->drn",
        attended,
        w_out.reshape(w_out.shape[0], n, -1),
        preferred_element_type=jnp.float32,
    ).astype(jnp.bfloat16)
    return sum_pieces(lax.all_to_all(partial, TENSOR, 0, 0, tiled=True))


def move_keyval(keyval):
    rows = keyval.shape[0]
    y_me = lax.axis_index("yh")
    pieces = [lax.ppermute(keyval, TENSOR, keyval_routes(k)) for k in range(N_Y)]
    stack = jnp.stack(pieces)
    roles = [lax.dynamic_index_in_dim(stack, (y_me - r) % N_Y, 0, False) for r in range(N_Y)]
    key = jnp.concatenate(roles[:2], axis=1).reshape(rows, 1, HD)
    value = jnp.concatenate(roles[2:], axis=1).reshape(rows, 1, HD)
    return key, value


def heads_of(features, labels, w_query, w_keyval):
    rows = features.shape[0]
    keyval = jnp.dot(features, w_keyval, preferred_element_type=jnp.float32).astype(jnp.bfloat16)
    key, value = move_keyval(keyval)
    query = jnp.dot(features, w_query, preferred_element_type=jnp.float32)
    positions, visible = doc_layout(labels)
    cosine, sine = rotation_tables(positions)
    query_rot = rotate(query.reshape(rows, 2, HD), cosine, sine).astype(jnp.bfloat16)
    key_rot = rotate(key.astype(jnp.float32), cosine, sine).astype(jnp.bfloat16)
    return attend(query_rot.reshape(rows, 1, 2, HD), key_rot, value, visible)


def to_all(rows, axes, n):
    sent = jnp.broadcast_to(rows[None], (n,) + rows.shape)
    return lax.all_to_all(sent, axes, 0, 0, tiled=True)


def shards(activations, w_query, w_keyval, w_out, targets, segments):
    block = lax.axis_index(DP)
    n_tensor = N_Z * N_Y

    kept = lax.all_gather(activations[:KEEP], "yh", axis=1, tiled=True)
    kept = lax.all_gather(kept, "z", axis=1, tiled=True)

    tails = to_all(activations[KEEP:], TENSOR, n_tensor)
    tails = tails.transpose(1, 0, 2).reshape(MOVE, -1)
    tail_docs = lax.dynamic_slice_in_dim(targets, block * MOVE, MOVE) // RECV
    tails = heads_of(tails, tail_docs, w_query, w_keyval)
    tails = scatter_sum(tails, w_out)

    slots = lax.iota(jnp.int32, RECV)
    wanted = targets - block * RECV
    select = (slots[:, None] == wanted[None, :]).astype(jnp.bfloat16)
    n_dp = targets.shape[0] // MOVE
    tails = to_all(tails, DP, n_dp).reshape(targets.shape[0], -1)
    arrived = jnp.dot(select, tails, preferred_element_type=jnp.float32).astype(jnp.bfloat16)

    kept = heads_of(kept, segments[:KEEP], w_query, w_keyval)
    kept = scatter_sum(kept, w_out)
    return jnp.concatenate([kept, arrived], axis=0)


def solution(mesh):
    fine = Mesh(
        mesh.devices.reshape(8, 2, 2, N_Z, N_Y), ("x", "yl", "core", "z", "yh")
    )
    placed = (
        P(DP, TENSOR),
        P(None, TENSOR),
        P(None, TENSOR),
        P(TENSOR, None),
        P(),
        P(DP),
    )
    return jax.shard_map(
        shards, mesh=fine, in_specs=placed, out_specs=P(DP, TENSOR), check_vma=False
    )
```

```python
import math

import jax
import jax.numpy as jnp
from jax import lax
from jax.experimental import pallas as pl
from jax.experimental.pallas import tpu as pltpu
from jax.sharding import Mesh
from jax.sharding import PartitionSpec as P

HQ = 64
KVH = 8
HD = 128
KEEP = 96
MOVE = 32
RECV = 64
SEQ = 128

N_Z = 8
N_Y = 4
DP = ("x", "yl", "core")
TENSOR = ("z", "yh")

rope_base = 500000.0


def rotation_tables(positions):
    half = HD // 2
    freqs = rope_base ** (-(jnp.arange(half, dtype=jnp.float32) * 2.0 / HD))
    angles = positions.astype(jnp.float32)[:, None] * freqs[None, :]
    return (jnp.cos(angles), jnp.sin(angles))


def rotate(values, cosine, sine):
    half = HD // 2
    first = values[..., :half]
    second = values[..., half:]
    cosine = cosine[:, None, :]
    sine = sine[:, None, :]
    return jnp.concatenate(
        [first * cosine - second * sine, second * cosine + first * sine], axis=-1
    )


def doc_layout(segment):
    same = segment[:, None] == segment[None, :]
    indices = jnp.arange(segment.shape[0])
    earlier = indices[None, :] < indices[:, None]
    positions = jnp.sum(jnp.logical_and(same, earlier), axis=1)
    visible = jnp.logical_and(same, indices[None, :] <= indices[:, None])
    return (positions, visible)


def attend(query_rot, key_rot, value_rows, visible):
    count = query_rot.shape[0]
    scores = jnp.einsum(
        "rkgd,ckd->kgrc", query_rot, key_rot, preferred_element_type=jnp.float32
    ) / math.sqrt(HD)
    scores = jnp.where(visible[None, None], scores, -1e30)
    top = jnp.max(scores, axis=-1, keepdims=True)
    expd = jnp.exp(scores - top)
    weights = (expd / jnp.sum(expd, axis=-1, keepdims=True)).astype(jnp.bfloat16)
    result = jnp.einsum("kgrc,ckd->rkgd", weights, value_rows, preferred_element_type=jnp.float32)
    return result.astype(jnp.bfloat16).reshape(count, -1)


def ring(n, k):
    return [(i, (i + k) % n) for i in range(n)]


def move_keyval(keyval):
    rows = keyval.shape[0]
    y_me = lax.axis_index("yh")
    other = lax.ppermute(keyval, "yh", [(i, i ^ 1) for i in range(N_Y)])
    low = y_me % 2 == 0
    whole = jnp.concatenate(
        [jnp.where(low, keyval, other), jnp.where(low, other, keyval)], axis=1
    )
    half = N_Z * N_Y // 2

    def routes(flip):
        return [
            (s, N_Y * ((s % half) // 2) + s % 2 + 2 * ((s // half) ^ flip)) for s in range(2 * half)
        ]

    straight = lax.ppermute(whole, TENSOR, routes(0))
    crossed = lax.ppermute(whole, TENSOR, routes(1))
    first = y_me < 2
    key = jnp.where(first, straight, crossed)
    value = jnp.where(first, crossed, straight)
    return key.reshape(rows, 1, HD), value.reshape(rows, 1, HD)


def sum_pieces(pieces):
    return jnp.sum(pieces.astype(jnp.float32), axis=0).astype(jnp.bfloat16)


def output_kernel(attended_ref, w_ref, kept_ref, tail_ref):
    rows = jnp.dot(attended_ref[...], w_ref[...], preferred_element_type=jnp.float32)
    rows = rows.astype(jnp.bfloat16)
    kept_ref[...] = rows[:KEEP]
    width = tail_ref.shape[2]
    for d in range(tail_ref.shape[0]):
        tail_ref[d] = rows[KEEP:, d * width : (d + 1) * width]


def output_partials(attended, w_out):
    depth, wide = w_out.shape
    n = N_Z * N_Y
    return pl.pallas_call(
        output_kernel,
        grid=(N_Z,),
        in_specs=[
            pl.BlockSpec((KEEP + MOVE, depth), lambda i: (0, 0)),
            pl.BlockSpec((depth, wide // N_Z), lambda i: (0, i)),
        ],
        out_specs=[
            pl.BlockSpec((KEEP, wide // N_Z), lambda i: (0, i)),
            pl.BlockSpec((N_Y, MOVE, wide // n), lambda i: (i, 0, 0)),
        ],
        out_shape=[
            jax.ShapeDtypeStruct((KEEP, wide), jnp.bfloat16),
            jax.ShapeDtypeStruct((n, MOVE, wide // n), jnp.bfloat16),
        ],
        compiler_params=pltpu.CompilerParams(vmem_limit_bytes=16 * 1024 * 1024),
    )(attended, w_out)


def sum_over_y(rows):
    me = lax.axis_index("yh")
    width = rows.shape[1] // N_Y

    def part(y):
        return lax.dynamic_slice_in_dim(rows, y * width, width, 1)

    near, far = me ^ 1, me ^ 2
    sent = jnp.concatenate([part(near), part(near ^ 2)], axis=1)
    held = jnp.concatenate([part(me), part(far)], axis=1)
    got = lax.ppermute(sent, "yh", [(i, i ^ 1) for i in range(N_Y)])
    held = held.astype(jnp.float32) + got.astype(jnp.float32)
    got = lax.ppermute(
        held[:, width:].astype(jnp.bfloat16), "yh", [(i, i ^ 2) for i in range(N_Y)]
    )
    return (held[:, :width] + got.astype(jnp.float32)).astype(jnp.bfloat16)


def shards(activations, w_query, w_keyval, w_out, targets, segments):
    block = lax.axis_index(DP)
    tail_docs = lax.dynamic_slice_in_dim(targets, block * MOVE, MOVE) // RECV
    labels = jnp.concatenate([segments[:KEEP], -1 - tail_docs])
    positions, visible = doc_layout(labels)
    cosine, sine = rotation_tables(positions)

    z_me = lax.axis_index("z")
    own = lax.all_gather(activations, "yh", axis=1, tiled=True)
    depth = own.shape[1]

    def times(weight, chunk, k):
        rows = lax.dynamic_slice_in_dim(weight, ((z_me + k) % N_Z) * depth, depth, 0)
        return jnp.dot(chunk, rows, preferred_element_type=jnp.float32)

    query = times(w_query, own, 0)
    keyval = times(w_keyval, own, 0)
    up, down = own, own
    for step in range(1, N_Z // 2):
        up = lax.ppermute(up, "z", ring(N_Z, 1))
        down = lax.ppermute(down, "z", ring(N_Z, -1))
        query = query + times(w_query, up, -step) + times(w_query, down, step)
        keyval = keyval + times(w_keyval, up, -step) + times(w_keyval, down, step)
    half = SEQ // 2
    up = lax.ppermute(up[:half], "z", ring(N_Z, 1))
    down = lax.ppermute(down[half:], "z", ring(N_Z, -1))
    last = jnp.concatenate([up, down], axis=0)
    keyval = (keyval + times(w_keyval, last, N_Z // 2)).astype(jnp.bfloat16)
    key, value = move_keyval(keyval)
    query = query + times(w_query, last, N_Z // 2)

    query_rot = rotate(query.reshape(SEQ, 2, HD), cosine, sine).astype(jnp.bfloat16)
    key_rot = rotate(key.astype(jnp.float32), cosine, sine).astype(jnp.bfloat16)
    attended = attend(query_rot.reshape(SEQ, 1, 2, HD), key_rot, value, visible)

    kept, moving = output_partials(attended, w_out)
    kept = lax.psum_scatter(kept.T, "z", scatter_dimension=0, tiled=True)
    moving = sum_pieces(lax.all_to_all(moving, TENSOR, 0, 0, tiled=True))
    kept = sum_over_y(kept.T)

    slots = lax.iota(jnp.int32, RECV)
    wanted = targets - block * RECV
    select = (slots[:, None] == wanted[None, :]).astype(jnp.bfloat16)
    tails = jnp.broadcast_to(moving[None], (targets.shape[0] // MOVE,) + moving.shape)
    tails = lax.all_to_all(tails, DP, 0, 0, tiled=True).reshape(targets.shape[0], -1)
    arrived = jnp.dot(select, tails, preferred_element_type=jnp.float32).astype(jnp.bfloat16)
    return jnp.concatenate([kept, arrived], axis=0)


def solution(mesh):
    fine = Mesh(
        mesh.devices.reshape(8, 2, 2, N_Z, N_Y), ("x", "yl", "core", "z", "yh")
    )
    placed = (
        P(DP, TENSOR),
        P(None, TENSOR),
        P(None, TENSOR),
        P(TENSOR, None),
        P(),
        P(DP),
    )
    return jax.shard_map(
        shards, mesh=fine, in_specs=placed, out_specs=P(DP, TENSOR), check_vma=False
    )
```

```python
import functools
import math

import jax
import jax.numpy as jnp
from jax import lax
from jax.experimental import pallas as pl
from jax.experimental.pallas import tpu as pltpu
from jax.sharding import Mesh
from jax.sharding import PartitionSpec as P

HQ = 64
KVH = 8
HD = 128
KEEP = 96
MOVE = 32
RECV = 64
SEQ = 128

N_Z = 8
N_Y = 4
DISTANCES = (0, -1, 1, -2, 2, -3, 3)
DP = ("x", "yl", "core")
TENSOR = ("z", "yh")

rope_base = 500000.0


def rotation_tables(positions):
    half = HD // 2
    freqs = rope_base ** (-(jnp.arange(half, dtype=jnp.float32) * 2.0 / HD))
    angles = positions.astype(jnp.float32)[:, None] * freqs[None, :]
    return (jnp.cos(angles), jnp.sin(angles))


def rotate(values, cosine, sine):
    half = HD // 2
    first = values[..., :half]
    second = values[..., half:]
    cosine = cosine[:, None, :]
    sine = sine[:, None, :]
    return jnp.concatenate(
        [first * cosine - second * sine, second * cosine + first * sine], axis=-1
    )


def doc_layout(segment):
    same = segment[:, None] == segment[None, :]
    indices = jnp.arange(segment.shape[0])
    earlier = indices[None, :] < indices[:, None]
    positions = jnp.sum(jnp.logical_and(same, earlier), axis=1)
    visible = jnp.logical_and(same, indices[None, :] <= indices[:, None])
    return (positions, visible)


def attend(query_rot, key_rot, value_rows, visible):
    count = query_rot.shape[0]
    scores = jnp.einsum(
        "rkgd,ckd->kgrc", query_rot, key_rot, preferred_element_type=jnp.float32
    ) / math.sqrt(HD)
    scores = jnp.where(visible[None, None], scores, -1e30)
    top = jnp.max(scores, axis=-1, keepdims=True)
    expd = jnp.exp(scores - top)
    weights = (expd / jnp.sum(expd, axis=-1, keepdims=True)).astype(jnp.bfloat16)
    result = jnp.einsum("kgrc,ckd->rkgd", weights, value_rows, preferred_element_type=jnp.float32)
    return result.astype(jnp.bfloat16).reshape(count, -1)


def ring(n, k):
    return [(i, (i + k) % n) for i in range(n)]


def move_keyval(keyval):
    rows = keyval.shape[0]
    y_me = lax.axis_index("yh")
    other = lax.ppermute(keyval, "yh", [(i, i ^ 1) for i in range(N_Y)])
    low = y_me % 2 == 0
    whole = jnp.concatenate(
        [jnp.where(low, keyval, other), jnp.where(low, other, keyval)], axis=1
    )
    half = N_Z * N_Y // 2

    def routes(flip):
        return [
            (s, N_Y * ((s % half) // 2) + s % 2 + 2 * ((s // half) ^ flip)) for s in range(2 * half)
        ]

    straight = lax.ppermute(whole, TENSOR, routes(0))
    crossed = lax.ppermute(whole, TENSOR, routes(1))
    first = y_me < 2
    key = jnp.where(first, straight, crossed)
    value = jnp.where(first, crossed, straight)
    return key.reshape(rows, 1, HD), value.reshape(rows, 1, HD)


def sum_pieces(pieces):
    return jnp.sum(pieces.astype(jnp.float32), axis=0).astype(jnp.bfloat16)


def output_kernel(attended_ref, w_ref, kept_ref, tail_ref):
    rows = jnp.dot(attended_ref[...], w_ref[...], preferred_element_type=jnp.float32)
    rows = rows.astype(jnp.bfloat16)
    kept_ref[...] = rows[:KEEP]
    width = tail_ref.shape[2]
    for d in range(tail_ref.shape[0]):
        tail_ref[d] = rows[KEEP:, d * width : (d + 1) * width]


def output_partials(attended, w_out):
    depth, wide = w_out.shape
    n = N_Z * N_Y
    return pl.pallas_call(
        output_kernel,
        grid=(N_Z,),
        in_specs=[
            pl.BlockSpec((KEEP + MOVE, depth), lambda i: (0, 0)),
            pl.BlockSpec((depth, wide // N_Z), lambda i: (0, i)),
        ],
        out_specs=[
            pl.BlockSpec((KEEP, wide // N_Z), lambda i: (0, i)),
            pl.BlockSpec((N_Y, MOVE, wide // n), lambda i: (i, 0, 0)),
        ],
        out_shape=[
            jax.ShapeDtypeStruct((KEEP, wide), jnp.bfloat16),
            jax.ShapeDtypeStruct((n, MOVE, wide // n), jnp.bfloat16),
        ],
        compiler_params=pltpu.CompilerParams(vmem_limit_bytes=16 * 1024 * 1024),
    )(attended, pltpu.with_memory_space_constraint(w_out, pltpu.HBM))


def sum_over_y(rows):
    me = lax.axis_index("yh")
    width = rows.shape[1] // N_Y

    def part(y):
        return lax.dynamic_slice_in_dim(rows, y * width, width, 1)

    near, far = me ^ 1, me ^ 2
    sent = jnp.concatenate([part(near), part(near ^ 2)], axis=1)
    held = jnp.concatenate([part(me), part(far)], axis=1)
    got = lax.ppermute(sent, "yh", [(i, i ^ 1) for i in range(N_Y)])
    held = held.astype(jnp.float32) + got.astype(jnp.float32)
    got = lax.ppermute(
        held[:, width:].astype(jnp.bfloat16), "yh", [(i, i ^ 2) for i in range(N_Y)]
    )
    return (held[:, :width] + got.astype(jnp.float32)).astype(jnp.bfloat16)


def product_kernel(transposed, z_ref, *refs):
    *piece_refs, w_ref, out_ref = refs
    depth = piece_refs[0].shape[1]

    def times(piece, k):
        at = pl.multiple_of(lax.rem(z_ref[0] + k + N_Z, N_Z) * depth, depth)
        if transposed:
            w = w_ref[:, pl.ds(at, depth)]
        else:
            w = w_ref[pl.ds(at, depth), :]
        return lax.dot_general(
            piece[...],
            w,
            (((1,), (1 if transposed else 0,)), ((), ())),
            preferred_element_type=jnp.float32,
        )

    total = jnp.concatenate(
        [times(piece_refs[-2], N_Z // 2), times(piece_refs[-1], N_Z // 2)], axis=0
    )
    for piece, k in zip(piece_refs[:-2], DISTANCES, strict=True):
        total = total + times(piece, k)
    out_ref[...] = total.astype(out_ref.dtype)


def product(pieces, weight, transposed, dtype):
    rows = pieces[0].shape[0]
    columns = weight.shape[0] if transposed else weight.shape[1]
    z_me = lax.axis_index("z").reshape(1)
    return pl.pallas_call(
        functools.partial(product_kernel, transposed),
        in_specs=[pl.BlockSpec(memory_space=pltpu.SMEM)]
        + [pl.BlockSpec(memory_space=pltpu.VMEM)] * (len(pieces) + 1),
        out_specs=pl.BlockSpec(memory_space=pltpu.VMEM),
        out_shape=jax.ShapeDtypeStruct((rows, columns), dtype),
        compiler_params=pltpu.CompilerParams(vmem_limit_bytes=24 * 1024 * 1024),
    )(z_me, *pieces, weight)


def shards(activations, w_query, w_keyval, w_out, targets, segments):
    block = lax.axis_index(DP)
    tail_docs = lax.dynamic_slice_in_dim(targets, block * MOVE, MOVE) // RECV
    labels = jnp.concatenate([segments[:KEEP], -1 - tail_docs])
    positions, visible = doc_layout(labels)
    cosine, sine = rotation_tables(positions)

    own = lax.all_gather(activations, "yh", axis=1, tiled=True)
    pieces = [own]
    up, down = own, own
    for _ in range(1, N_Z // 2):
        up = lax.ppermute(up, "z", ring(N_Z, 1))
        down = lax.ppermute(down, "z", ring(N_Z, -1))
        pieces += [up, down]
    half = SEQ // 2
    pieces.append(lax.ppermute(up[:half], "z", ring(N_Z, 1)))
    pieces.append(lax.ppermute(down[half:], "z", ring(N_Z, -1)))
    keyval = product(pieces, w_keyval.T, True, jnp.bfloat16)
    key, value = move_keyval(keyval)
    query = product(pieces, w_query, False, jnp.float32)

    query_rot = rotate(query.reshape(SEQ, 2, HD), cosine, sine).astype(jnp.bfloat16)
    key_rot = rotate(key.astype(jnp.float32), cosine, sine).astype(jnp.bfloat16)
    attended = attend(query_rot.reshape(SEQ, 1, 2, HD), key_rot, value, visible)

    kept, moving = output_partials(attended, w_out)
    kept = lax.psum_scatter(kept.T, "z", scatter_dimension=0, tiled=True)
    moving = sum_pieces(lax.all_to_all(moving, TENSOR, 0, 0, tiled=True))
    kept = sum_over_y(kept.T)

    slots = lax.iota(jnp.int32, RECV)
    wanted = targets - block * RECV
    select = (slots[:, None] == wanted[None, :]).astype(jnp.bfloat16)
    tails = jnp.broadcast_to(moving[None], (targets.shape[0] // MOVE,) + moving.shape)
    tails = lax.all_to_all(tails, DP, 0, 0, tiled=True).reshape(targets.shape[0], -1)
    arrived = jnp.dot(select, tails, preferred_element_type=jnp.float32).astype(jnp.bfloat16)
    return jnp.concatenate([kept, arrived], axis=0)


def solution(mesh):
    fine = Mesh(
        mesh.devices.reshape(8, 2, 2, N_Z, N_Y), ("x", "yl", "core", "z", "yh")
    )
    placed = (
        P(DP, TENSOR),
        P(None, TENSOR),
        P(None, TENSOR),
        P(TENSOR, None),
        P(),
        P(DP),
    )
    return jax.shard_map(
        shards, mesh=fine, in_specs=placed, out_specs=P(DP, TENSOR), check_vma=False
    )
```

```python
import functools
import math

import jax
import jax.numpy as jnp
from jax import lax
from jax.experimental import pallas as pl
from jax.experimental.pallas import tpu as pltpu
from jax.sharding import Mesh
from jax.sharding import PartitionSpec as P

HQ = 64
KVH = 8
HD = 128
KEEP = 96
MOVE = 32
RECV = 64
SEQ = 128

N_Z = 8
N_Y = 4
DISTANCES = (0, -1, 1, -2, 2, -3, 3)
DP = ("x", "yl", "core")
TENSOR = ("z", "yh")

rope_base = 500000.0


def rotation_tables(positions):
    half = HD // 2
    freqs = rope_base ** (-(jnp.arange(half, dtype=jnp.float32) * 2.0 / HD))
    angles = positions.astype(jnp.float32)[:, None] * freqs[None, :]
    return (jnp.cos(angles), jnp.sin(angles))


def rotate(values, cosine, sine):
    half = HD // 2
    first = values[..., :half]
    second = values[..., half:]
    cosine = cosine[:, None, :]
    sine = sine[:, None, :]
    return jnp.concatenate(
        [first * cosine - second * sine, second * cosine + first * sine], axis=-1
    )


def doc_layout(segment):
    same = segment[:, None] == segment[None, :]
    indices = jnp.arange(segment.shape[0])
    earlier = indices[None, :] < indices[:, None]
    positions = jnp.sum(jnp.logical_and(same, earlier), axis=1)
    visible = jnp.logical_and(same, indices[None, :] <= indices[:, None])
    return (positions, visible)


def attend(query_rot, key_rot, value_rows, visible):
    count = query_rot.shape[0]
    scores = jnp.einsum(
        "rkgd,ckd->kgrc", query_rot, key_rot, preferred_element_type=jnp.float32
    ) / math.sqrt(HD)
    scores = jnp.where(visible[None, None], scores, -1e30)
    top = jnp.max(scores, axis=-1, keepdims=True)
    expd = jnp.exp(scores - top)
    weights = (expd / jnp.sum(expd, axis=-1, keepdims=True)).astype(jnp.bfloat16)
    result = jnp.einsum("kgrc,ckd->rkgd", weights, value_rows, preferred_element_type=jnp.float32)
    return result.astype(jnp.bfloat16).reshape(count, -1)


def ring(n, k):
    return [(i, (i + k) % n) for i in range(n)]


def move_keyval(keyval):
    rows = keyval.shape[0]
    y_me = lax.axis_index("yh")
    other = lax.ppermute(keyval, "yh", [(i, i ^ 1) for i in range(N_Y)])
    low = y_me % 2 == 0
    whole = jnp.concatenate(
        [jnp.where(low, keyval, other), jnp.where(low, other, keyval)], axis=1
    )
    half = N_Z * N_Y // 2

    def routes(flip):
        return [
            (s, N_Y * ((s % half) // 2) + s % 2 + 2 * ((s // half) ^ flip)) for s in range(2 * half)
        ]

    straight = lax.ppermute(whole, TENSOR, routes(0))
    crossed = lax.ppermute(whole, TENSOR, routes(1))
    first = y_me < 2
    key = jnp.where(first, straight, crossed)
    value = jnp.where(first, crossed, straight)
    return key.reshape(rows, 1, HD), value.reshape(rows, 1, HD)


def sum_pieces(pieces):
    return jnp.sum(pieces.astype(jnp.float32), axis=0).astype(jnp.bfloat16)


def output_kernel(
    z_ref, attended_ref, w_ref, kept_ref, up_ref, down_ref, tail_ref, held, sems
):
    wide = kept_ref.shape[2]
    width = tail_ref.shape[2]
    copies = [
        pltpu.make_async_copy(w_ref.at[:, pl.ds(z * wide, wide)], held.at[z], sems.at[z])
        for z in range(N_Z)
    ]
    for copy in copies:
        copy.start()
    for z in range(N_Z):
        copies[z].wait()
        rows = jnp.dot(attended_ref[...], held[z], preferred_element_type=jnp.float32)
        rows = rows.astype(jnp.bfloat16)
        kept_ref[z] = rows[:KEEP]
        for y in range(N_Y):
            tail_ref[z * N_Y + y] = rows[KEEP:, y * width : (y + 1) * width]
    far = lax.rem(z_ref[0] + N_Z // 2, N_Z)
    up_ref[...] = kept_ref[far, : KEEP // 2]
    down_ref[...] = kept_ref[far, KEEP // 2 :]


def output_partials(attended, w_out):
    depth, columns = w_out.shape
    wide = columns // N_Z
    n = N_Z * N_Y
    vmem = pl.BlockSpec(memory_space=pltpu.VMEM)
    return pl.pallas_call(
        output_kernel,
        in_specs=[
            pl.BlockSpec(memory_space=pltpu.SMEM),
            vmem,
            pl.BlockSpec(memory_space=pl.ANY),
        ],
        out_specs=[vmem] * 4,
        out_shape=[
            jax.ShapeDtypeStruct((N_Z, KEEP, wide), jnp.bfloat16),
            jax.ShapeDtypeStruct((KEEP // 2, wide), jnp.bfloat16),
            jax.ShapeDtypeStruct((KEEP // 2, wide), jnp.bfloat16),
            jax.ShapeDtypeStruct((n, MOVE, columns // n), jnp.bfloat16),
        ],
        scratch_shapes=[
            pltpu.VMEM((N_Z, depth, wide), jnp.bfloat16),
            pltpu.SemaphoreType.DMA((N_Z,)),
        ],
        compiler_params=pltpu.CompilerParams(vmem_limit_bytes=32 * 1024 * 1024),
    )(
        lax.axis_index("z").reshape(1),
        attended,
        pltpu.with_memory_space_constraint(w_out, pltpu.HBM),
    )


def hop_kernel(k, z_ref, up_ref, down_ref, parts_ref, up_out, down_out):
    above = parts_ref.at[lax.rem(z_ref[0] + k, N_Z)]
    below = parts_ref.at[lax.rem(z_ref[0] + N_Z - k, N_Z)]
    n, got = parts_ref.shape[1], up_ref.shape[0]

    def add(a, b):
        return (a.astype(jnp.float32) + b.astype(jnp.float32)).astype(jnp.bfloat16)

    up_out[:got] = add(above[:got], up_ref[...])
    down_out[n - got :] = add(below[n - got :], down_ref[...])
    if got < n:
        up_out[got:] = above[got:]
        down_out[: n - got] = below[: n - got]


def end_kernel(at_ref, up_ref, down_ref, parts_ref, sent_ref, held_ref, total):
    own = parts_ref.at[at_ref[0]]
    total[...] = (
        own[...].astype(jnp.float32)
        + up_ref[...].astype(jnp.float32)
        + down_ref[...].astype(jnp.float32)
    )
    me = at_ref[1]
    width = total.shape[1] // N_Y

    def part(y):
        return total[:, pl.ds(pl.multiple_of(y * width, width), width)]

    sent_ref[:, :width] = part(me ^ 1).astype(jnp.bfloat16)
    sent_ref[:, width:] = part(me ^ 3).astype(jnp.bfloat16)
    held_ref[:, :width] = part(me)
    held_ref[:, width:] = part(me ^ 2)


def scatter_sum_kept(parts, up, down):
    n, wide = parts.shape[1:]
    z_me = lax.axis_index("z").reshape(1)
    vmem, smem = pl.BlockSpec(memory_space=pltpu.VMEM), pl.BlockSpec(memory_space=pltpu.SMEM)
    params = pltpu.CompilerParams(vmem_limit_bytes=16 * 1024 * 1024)
    for k in range(N_Z // 2 - 1, -1, -1):
        up = lax.ppermute(up, "z", ring(N_Z, 1))
        down = lax.ppermute(down, "z", ring(N_Z, -1))
        if k:
            up, down = pl.pallas_call(
                functools.partial(hop_kernel, k),
                in_specs=[smem, vmem, vmem, vmem],
                out_specs=[vmem] * 2,
                out_shape=[jax.ShapeDtypeStruct((n, wide), jnp.bfloat16)] * 2,
                compiler_params=params,
            )(z_me, up, down, parts)
    at = jnp.stack([lax.axis_index("z"), lax.axis_index("yh")])
    sent, held = pl.pallas_call(
        end_kernel,
        in_specs=[smem, vmem, vmem, vmem],
        out_specs=[vmem] * 2,
        out_shape=[
            jax.ShapeDtypeStruct((n, wide // 2), jnp.bfloat16),
            jax.ShapeDtypeStruct((n, wide // 2), jnp.float32),
        ],
        scratch_shapes=[pltpu.VMEM((n, wide), jnp.float32)],
        compiler_params=params,
    )(at, up, down, parts)
    width = wide // N_Y
    got = lax.ppermute(sent, "yh", [(i, i ^ 1) for i in range(N_Y)])
    held = held + got.astype(jnp.float32)
    got = lax.ppermute(
        held[:, width:].astype(jnp.bfloat16), "yh", [(i, i ^ 2) for i in range(N_Y)]
    )
    return (held[:, :width] + got.astype(jnp.float32)).astype(jnp.bfloat16)


def product_kernel(transposed, z_ref, *refs):
    *piece_refs, w_ref, out_ref = refs
    depth = piece_refs[0].shape[1]

    def times(piece, k):
        at = pl.multiple_of(lax.rem(z_ref[0] + k + N_Z, N_Z) * depth, depth)
        if transposed:
            w = w_ref[:, pl.ds(at, depth)]
        else:
            w = w_ref[pl.ds(at, depth), :]
        return lax.dot_general(
            piece[...],
            w,
            (((1,), (1 if transposed else 0,)), ((), ())),
            preferred_element_type=jnp.float32,
        )

    total = jnp.concatenate(
        [times(piece_refs[-2], N_Z // 2), times(piece_refs[-1], N_Z // 2)], axis=0
    )
    for piece, k in zip(piece_refs[:-2], DISTANCES, strict=True):
        total = total + times(piece, k)
    out_ref[...] = total.astype(out_ref.dtype)


def product(pieces, weight, transposed, dtype):
    rows = pieces[0].shape[0]
    columns = weight.shape[0] if transposed else weight.shape[1]
    z_me = lax.axis_index("z").reshape(1)
    return pl.pallas_call(
        functools.partial(product_kernel, transposed),
        in_specs=[pl.BlockSpec(memory_space=pltpu.SMEM)]
        + [pl.BlockSpec(memory_space=pltpu.VMEM)] * (len(pieces) + 1),
        out_specs=pl.BlockSpec(memory_space=pltpu.VMEM),
        out_shape=jax.ShapeDtypeStruct((rows, columns), dtype),
        compiler_params=pltpu.CompilerParams(vmem_limit_bytes=24 * 1024 * 1024),
    )(z_me, *pieces, weight)


def shards(activations, w_query, w_keyval, w_out, targets, segments):
    block = lax.axis_index(DP)
    tail_docs = lax.dynamic_slice_in_dim(targets, block * MOVE, MOVE) // RECV
    labels = jnp.concatenate([segments[:KEEP], -1 - tail_docs])
    positions, visible = doc_layout(labels)
    cosine, sine = rotation_tables(positions)

    own = lax.all_gather(activations, "yh", axis=1, tiled=True)
    pieces = [own]
    up, down = own, own
    for _ in range(1, N_Z // 2):
        up = lax.ppermute(up, "z", ring(N_Z, 1))
        down = lax.ppermute(down, "z", ring(N_Z, -1))
        pieces += [up, down]
    half = SEQ // 2
    pieces.append(lax.ppermute(up[:half], "z", ring(N_Z, 1)))
    pieces.append(lax.ppermute(down[half:], "z", ring(N_Z, -1)))
    keyval = product(pieces, w_keyval.T, True, jnp.bfloat16)
    key, value = move_keyval(keyval)
    query = product(pieces, w_query, False, jnp.float32)

    query_rot = rotate(query.reshape(SEQ, 2, HD), cosine, sine).astype(jnp.bfloat16)
    key_rot = rotate(key.astype(jnp.float32), cosine, sine).astype(jnp.bfloat16)
    attended = attend(query_rot.reshape(SEQ, 1, 2, HD), key_rot, value, visible)

    kept, up, down, moving = output_partials(attended, w_out)
    moving = sum_pieces(lax.all_to_all(moving, TENSOR, 0, 0, tiled=True))
    kept = scatter_sum_kept(kept, up, down)

    slots = lax.iota(jnp.int32, RECV)
    wanted = targets - block * RECV
    select = (slots[:, None] == wanted[None, :]).astype(jnp.bfloat16)
    tails = jnp.broadcast_to(moving[None], (targets.shape[0] // MOVE,) + moving.shape)
    tails = lax.all_to_all(tails, DP, 0, 0, tiled=True).reshape(targets.shape[0], -1)
    arrived = jnp.dot(select, tails, preferred_element_type=jnp.float32).astype(jnp.bfloat16)
    return jnp.concatenate([kept, arrived], axis=0)


def solution(mesh):
    fine = Mesh(
        mesh.devices.reshape(8, 2, 2, N_Z, N_Y), ("x", "yl", "core", "z", "yh")
    )
    placed = (
        P(DP, TENSOR),
        P(None, TENSOR),
        P(None, TENSOR),
        P(TENSOR, None),
        P(),
        P(DP),
    )
    return jax.shard_map(
        shards, mesh=fine, in_specs=placed, out_specs=P(DP, TENSOR), check_vma=False
    )
```

```python
import functools
import math

import jax
import jax.numpy as jnp
from jax import lax
from jax.experimental import pallas as pl
from jax.experimental.pallas import tpu as pltpu
from jax.sharding import Mesh
from jax.sharding import PartitionSpec as P

HQ = 64
KVH = 8
HD = 128
KEEP = 96
MOVE = 32
RECV = 64
SEQ = 128

N_Z = 8
N_Y = 4
DISTANCES = (0, -1, 1, -2, 2, -3, 3)
DP = ("x", "yl", "core")
TENSOR = ("z", "yh")

rope_base = 500000.0


def rotation_tables(positions):
    half = HD // 2
    freqs = rope_base ** (-(jnp.arange(half, dtype=jnp.float32) * 2.0 / HD))
    angles = positions.astype(jnp.float32)[:, None] * freqs[None, :]
    return (jnp.cos(angles), jnp.sin(angles))


def rotate(values, cosine, sine):
    half = HD // 2
    first = values[..., :half]
    second = values[..., half:]
    cosine = cosine[:, None, :]
    sine = sine[:, None, :]
    return jnp.concatenate(
        [first * cosine - second * sine, second * cosine + first * sine], axis=-1
    )


def doc_layout(segment):
    same = segment[:, None] == segment[None, :]
    indices = jnp.arange(segment.shape[0])
    earlier = indices[None, :] < indices[:, None]
    positions = jnp.sum(jnp.logical_and(same, earlier), axis=1)
    visible = jnp.logical_and(same, indices[None, :] <= indices[:, None])
    return (positions, visible)


def attend(query_rot, key_rot, value_rows, visible):
    count = query_rot.shape[0]
    scores = jnp.einsum(
        "rkgd,ckd->kgrc", query_rot, key_rot, preferred_element_type=jnp.float32
    ) / math.sqrt(HD)
    scores = jnp.where(visible[None, None], scores, -1e30)
    top = jnp.max(scores, axis=-1, keepdims=True)
    expd = jnp.exp(scores - top)
    weights = (expd / jnp.sum(expd, axis=-1, keepdims=True)).astype(jnp.bfloat16)
    result = jnp.einsum("kgrc,ckd->rkgd", weights, value_rows, preferred_element_type=jnp.float32)
    return result.astype(jnp.bfloat16).reshape(count, -1)


def ring(n, k):
    return [(i, (i + k) % n) for i in range(n)]


def move_keyval(keyval):
    rows = keyval.shape[0]
    y_me = lax.axis_index("yh")
    other = lax.ppermute(keyval, "yh", [(i, i ^ 1) for i in range(N_Y)])
    low = y_me % 2 == 0
    whole = jnp.concatenate(
        [jnp.where(low, keyval, other), jnp.where(low, other, keyval)], axis=1
    )
    half = N_Z * N_Y // 2

    def routes(flip):
        return [
            (s, N_Y * ((s % half) // 2) + s % 2 + 2 * ((s // half) ^ flip)) for s in range(2 * half)
        ]

    straight = lax.ppermute(whole, TENSOR, routes(0))
    crossed = lax.ppermute(whole, TENSOR, routes(1))
    first = y_me < 2
    key = jnp.where(first, straight, crossed)
    value = jnp.where(first, crossed, straight)
    return key.reshape(rows, 1, HD), value.reshape(rows, 1, HD), whole


def sum_pieces(pieces):
    return jnp.sum(pieces.astype(jnp.float32), axis=0).astype(jnp.bfloat16)


def output_kernel(
    z_ref, attended_ref, w_ref, kept_ref, up_ref, down_ref, tail_ref, held, sems
):
    wide = kept_ref.shape[2]
    width = tail_ref.shape[2]
    copies = [
        pltpu.make_async_copy(w_ref.at[:, pl.ds(z * wide, wide)], held.at[z], sems.at[z])
        for z in range(N_Z)
    ]
    for copy in copies:
        copy.start()
    for z in range(N_Z):
        copies[z].wait()
        rows = jnp.dot(attended_ref[...], held[z], preferred_element_type=jnp.float32)
        rows = rows.astype(jnp.bfloat16)
        kept_ref[z] = rows[:KEEP]
        for y in range(N_Y):
            tail_ref[z * N_Y + y] = rows[KEEP:, y * width : (y + 1) * width]
    far = lax.rem(z_ref[0] + N_Z // 2, N_Z)
    up_ref[...] = kept_ref[far, : KEEP // 2]
    down_ref[...] = kept_ref[far, KEEP // 2 :]


def output_partials(attended, w_out):
    depth, columns = w_out.shape
    wide = columns // N_Z
    n = N_Z * N_Y
    vmem = pl.BlockSpec(memory_space=pltpu.VMEM)
    return pl.pallas_call(
        output_kernel,
        in_specs=[
            pl.BlockSpec(memory_space=pltpu.SMEM),
            vmem,
            pl.BlockSpec(memory_space=pl.ANY),
        ],
        out_specs=[vmem] * 4,
        out_shape=[
            jax.ShapeDtypeStruct((N_Z, KEEP, wide), jnp.bfloat16),
            jax.ShapeDtypeStruct((KEEP // 2, wide), jnp.bfloat16),
            jax.ShapeDtypeStruct((KEEP // 2, wide), jnp.bfloat16),
            jax.ShapeDtypeStruct((n, MOVE, columns // n), jnp.bfloat16),
        ],
        scratch_shapes=[
            pltpu.VMEM((N_Z, depth, wide), jnp.bfloat16),
            pltpu.SemaphoreType.DMA((N_Z,)),
        ],
        compiler_params=pltpu.CompilerParams(vmem_limit_bytes=32 * 1024 * 1024),
    )(
        lax.axis_index("z").reshape(1),
        attended,
        pltpu.with_memory_space_constraint(w_out, pltpu.HBM),
    )


def hop_kernel(k, z_ref, after_ref, up_ref, down_ref, parts_ref, up_out, down_out):
    above = parts_ref.at[lax.rem(z_ref[0] + k, N_Z)]
    below = parts_ref.at[lax.rem(z_ref[0] + N_Z - k, N_Z)]
    n, got = parts_ref.shape[1], up_ref.shape[0]

    def add(a, b):
        return (a.astype(jnp.float32) + b.astype(jnp.float32)).astype(jnp.bfloat16)

    up_out[:got] = add(above[:got], up_ref[...])
    down_out[n - got :] = add(below[n - got :], down_ref[...])
    if got < n:
        up_out[got:] = above[got:]
        down_out[: n - got] = below[: n - got]


def end_kernel(z_ref, after_ref, up_ref, down_ref, parts_ref, out_ref):
    own = parts_ref.at[z_ref[0]]
    total = (
        own[...].astype(jnp.float32)
        + up_ref[...].astype(jnp.float32)
        + down_ref[...].astype(jnp.float32)
    ).astype(jnp.bfloat16)
    width = out_ref.shape[2]
    for y in range(N_Y):
        out_ref[y] = total[:, y * width : (y + 1) * width]


def spread_kernel(after_ref, pieces_ref, out_ref):
    total = jnp.sum(pieces_ref[...].astype(jnp.float32), axis=0).astype(jnp.bfloat16)
    for d in range(out_ref.shape[0]):
        out_ref[d] = total


def spread_sum(pieces, copies, after):
    vmem = pl.BlockSpec(memory_space=pltpu.VMEM)
    return pl.pallas_call(
        spread_kernel,
        in_specs=[pl.BlockSpec(memory_space=pl.ANY), vmem],
        out_specs=vmem,
        out_shape=jax.ShapeDtypeStruct((copies,) + pieces.shape[1:], jnp.bfloat16),
        compiler_params=pltpu.CompilerParams(vmem_limit_bytes=16 * 1024 * 1024),
    )(after, pieces)


def scatter_sums(parts, up, down, moving, n_dp):
    n, wide = parts.shape[1:]
    z_me = lax.axis_index("z").reshape(1)
    vmem, smem = pl.BlockSpec(memory_space=pltpu.VMEM), pl.BlockSpec(memory_space=pltpu.SMEM)
    params = pltpu.CompilerParams(vmem_limit_bytes=16 * 1024 * 1024)
    anywhere = pl.BlockSpec(memory_space=pl.ANY)
    moving = lax.all_to_all(moving, TENSOR, 0, 0, tiled=True)
    tails = z_me
    for k in range(N_Z // 2 - 1, -1, -1):
        up = lax.ppermute(up, "z", ring(N_Z, 1))
        down = lax.ppermute(down, "z", ring(N_Z, -1))
        if k:
            up, down = pl.pallas_call(
                functools.partial(hop_kernel, k),
                in_specs=[smem, anywhere, vmem, vmem, vmem],
                out_specs=[vmem] * 2,
                out_shape=[jax.ShapeDtypeStruct((n, wide), jnp.bfloat16)] * 2,
                compiler_params=params,
            )(z_me, moving if k == N_Z // 2 - 2 else z_me, up, down, parts)
        if k == N_Z // 2 - 1:
            moving = spread_sum(moving, n_dp, up)
            tails = lax.all_to_all(moving, DP, 0, 0, tiled=True)
    parts = pl.pallas_call(
        end_kernel,
        in_specs=[smem, anywhere, vmem, vmem, vmem],
        out_specs=vmem,
        out_shape=jax.ShapeDtypeStruct((N_Y, n, wide // N_Y), jnp.bfloat16),
        compiler_params=params,
    )(z_me, tails, up, down, parts)
    return sum_pieces(lax.all_to_all(parts, "yh", 0, 0, tiled=True)), tails


def product_kernel(transposed, z_ref, after_ref, *refs):
    *piece_refs, w_ref, out_ref = refs
    depth = piece_refs[0].shape[1]

    def times(piece, k):
        at = pl.multiple_of(lax.rem(z_ref[0] + k + N_Z, N_Z) * depth, depth)
        if transposed:
            w = w_ref[:, pl.ds(at, depth)]
        else:
            w = w_ref[pl.ds(at, depth), :]
        return lax.dot_general(
            piece[...],
            w,
            (((1,), (1 if transposed else 0,)), ((), ())),
            preferred_element_type=jnp.float32,
        )

    total = jnp.concatenate(
        [times(piece_refs[-2], N_Z // 2), times(piece_refs[-1], N_Z // 2)], axis=0
    )
    for piece, k in zip(piece_refs[:-2], DISTANCES, strict=True):
        total = total + times(piece, k)
    out_ref[...] = total.astype(out_ref.dtype)


def product(pieces, weight, transposed, dtype, after):
    rows = pieces[0].shape[0]
    columns = weight.shape[0] if transposed else weight.shape[1]
    z_me = lax.axis_index("z").reshape(1)
    return pl.pallas_call(
        functools.partial(product_kernel, transposed),
        in_specs=[pl.BlockSpec(memory_space=pltpu.SMEM), pl.BlockSpec(memory_space=pl.ANY)]
        + [pl.BlockSpec(memory_space=pltpu.VMEM)] * (len(pieces) + 1),
        out_specs=pl.BlockSpec(memory_space=pltpu.VMEM),
        out_shape=jax.ShapeDtypeStruct((rows, columns), dtype),
        compiler_params=pltpu.CompilerParams(vmem_limit_bytes=24 * 1024 * 1024),
    )(z_me, after, *pieces, weight)


def shards(activations, w_query, w_keyval, w_out, targets, segments):
    block = lax.axis_index(DP)
    tail_docs = lax.dynamic_slice_in_dim(targets, block * MOVE, MOVE) // RECV
    labels = jnp.concatenate([segments[:KEEP], -1 - tail_docs])
    positions, visible = doc_layout(labels)
    cosine, sine = rotation_tables(positions)

    own = lax.all_gather(activations, "yh", axis=1, tiled=True)
    pieces = [own]
    up, down = own, own
    for _ in range(1, N_Z // 2):
        up = lax.ppermute(up, "z", ring(N_Z, 1))
        down = lax.ppermute(down, "z", ring(N_Z, -1))
        pieces += [up, down]
    half = SEQ // 2
    pieces.append(lax.ppermute(up[:half], "z", ring(N_Z, 1)))
    pieces.append(lax.ppermute(down[half:], "z", ring(N_Z, -1)))
    keyval = product(pieces, w_keyval.T, True, jnp.bfloat16, lax.axis_index("z").reshape(1))
    key, value, whole = move_keyval(keyval)
    query = product(pieces, w_query, False, jnp.float32, whole)

    query_rot = rotate(query.reshape(SEQ, 2, HD), cosine, sine).astype(jnp.bfloat16)
    key_rot = rotate(key.astype(jnp.float32), cosine, sine).astype(jnp.bfloat16)
    attended = attend(query_rot.reshape(SEQ, 1, 2, HD), key_rot, value, visible)

    kept, up, down, moving = output_partials(attended, w_out)
    kept, tails = scatter_sums(kept, up, down, moving, targets.shape[0] // MOVE)

    slots = lax.iota(jnp.int32, RECV)
    wanted = targets - block * RECV
    select = (slots[:, None] == wanted[None, :]).astype(jnp.bfloat16)
    tails = tails.reshape(targets.shape[0], -1)
    arrived = jnp.dot(select, tails, preferred_element_type=jnp.float32).astype(jnp.bfloat16)
    return jnp.concatenate([kept, arrived], axis=0)


def solution(mesh):
    fine = Mesh(
        mesh.devices.reshape(8, 2, 2, N_Z, N_Y), ("x", "yl", "core", "z", "yh")
    )
    placed = (
        P(DP, TENSOR),
        P(None, TENSOR),
        P(None, TENSOR),
        P(TENSOR, None),
        P(),
        P(DP),
    )
    return jax.shard_map(
        shards, mesh=fine, in_specs=placed, out_specs=P(DP, TENSOR), check_vma=False
    )
```

```python
import functools
import math

import jax
import jax.numpy as jnp
from jax import lax
from jax.experimental import pallas as pl
from jax.experimental.pallas import tpu as pltpu
from jax.sharding import Mesh
from jax.sharding import PartitionSpec as P

HQ = 64
KVH = 8
HD = 128
KEEP = 96
MOVE = 32
RECV = 64
SEQ = 128

N_Z = 8
N_Y = 4
DISTANCES = (0, -1, 1, -2, 2, -3, 3)
DP = ("x", "yl", "core")
TENSOR = ("z", "yh")

rope_base = 500000.0


def rotation_tables(positions):
    half = HD // 2
    freqs = rope_base ** (-(jnp.arange(half, dtype=jnp.float32) * 2.0 / HD))
    angles = positions.astype(jnp.float32)[:, None] * freqs[None, :]
    return (jnp.cos(angles), jnp.sin(angles))


def rotate(values, cosine, sine):
    half = HD // 2
    first = values[..., :half]
    second = values[..., half:]
    cosine = cosine[:, None, :]
    sine = sine[:, None, :]
    return jnp.concatenate(
        [first * cosine - second * sine, second * cosine + first * sine], axis=-1
    )


def doc_layout(segment):
    same = segment[:, None] == segment[None, :]
    indices = jnp.arange(segment.shape[0])
    earlier = indices[None, :] < indices[:, None]
    positions = jnp.sum(jnp.logical_and(same, earlier), axis=1)
    visible = jnp.logical_and(same, indices[None, :] <= indices[:, None])
    return (positions, visible)


def attend(query_rot, key_rot, value_rows, visible):
    count = query_rot.shape[0]
    scores = jnp.einsum(
        "rkgd,ckd->kgrc", query_rot, key_rot, preferred_element_type=jnp.float32
    ) / math.sqrt(HD)
    scores = jnp.where(visible[None, None], scores, -1e30)
    top = jnp.max(scores, axis=-1, keepdims=True)
    expd = jnp.exp(scores - top)
    weights = (expd / jnp.sum(expd, axis=-1, keepdims=True)).astype(jnp.bfloat16)
    result = jnp.einsum("kgrc,ckd->rkgd", weights, value_rows, preferred_element_type=jnp.float32)
    return result.astype(jnp.bfloat16).reshape(count, -1)


def ring(n, k):
    return [(i, (i + k) % n) for i in range(n)]


def move_keyval(keyval):
    rows = keyval.shape[0]
    y_me = lax.axis_index("yh")
    other = lax.ppermute(keyval, "yh", [(i, i ^ 1) for i in range(N_Y)])
    low = y_me % 2 == 0
    whole = jnp.concatenate(
        [jnp.where(low, keyval, other), jnp.where(low, other, keyval)], axis=1
    )
    half = N_Z * N_Y // 2

    def routes(flip):
        return [
            (s, N_Y * ((s % half) // 2) + s % 2 + 2 * ((s // half) ^ flip)) for s in range(2 * half)
        ]

    straight = lax.ppermute(whole, TENSOR, routes(0))
    crossed = lax.ppermute(whole, TENSOR, routes(1))
    first = y_me < 2
    key = jnp.where(first, straight, crossed)
    value = jnp.where(first, crossed, straight)
    return key.reshape(rows, 1, HD), value.reshape(rows, 1, HD), whole


def sum_pieces(pieces):
    return jnp.sum(pieces.astype(jnp.float32), axis=0).astype(jnp.bfloat16)


def output_kernel(attended_ref, w_ref, kept_ref, tail_ref, held, rows_held, sems, out_sems):
    wide = held.shape[2]
    width = tail_ref.shape[2]
    copies = [
        pltpu.make_async_copy(w_ref.at[:, pl.ds(z * wide, wide)], held.at[z], sems.at[z])
        for z in range(N_Z)
    ]
    outs = [
        pltpu.make_async_copy(
            rows_held.at[z], kept_ref.at[:, pl.ds(z * wide, wide)], out_sems.at[z]
        )
        for z in range(N_Z)
    ]
    for copy in copies:
        copy.start()
    for z in range(N_Z):
        copies[z].wait()
        rows = jnp.dot(attended_ref[...], held[z], preferred_element_type=jnp.float32)
        rows = rows.astype(jnp.bfloat16)
        rows_held[z] = rows[:KEEP]
        outs[z].start()
        for y in range(N_Y):
            tail_ref[z * N_Y + y] = rows[KEEP:, y * width : (y + 1) * width]
    for copy in outs:
        copy.wait()


def output_partials(attended, w_out):
    depth, columns = w_out.shape
    wide = columns // N_Z
    n = N_Z * N_Y
    vmem, anywhere = pl.BlockSpec(memory_space=pltpu.VMEM), pl.BlockSpec(memory_space=pl.ANY)
    return pl.pallas_call(
        output_kernel,
        in_specs=[vmem, anywhere],
        out_specs=[pl.BlockSpec(memory_space=pltpu.HBM), vmem],
        out_shape=[
            jax.ShapeDtypeStruct((KEEP, columns), jnp.bfloat16),
            jax.ShapeDtypeStruct((n, MOVE, columns // n), jnp.bfloat16),
        ],
        scratch_shapes=[
            pltpu.VMEM((N_Z, depth, wide), jnp.bfloat16),
            pltpu.VMEM((N_Z, KEEP, wide), jnp.bfloat16),
            pltpu.SemaphoreType.DMA((N_Z,)),
            pltpu.SemaphoreType.DMA((N_Z,)),
        ],
        compiler_params=pltpu.CompilerParams(vmem_limit_bytes=32 * 1024 * 1024),
    )(attended, pltpu.with_memory_space_constraint(w_out, pltpu.HBM))


def spread_kernel(pieces_ref, out_ref):
    total = jnp.sum(pieces_ref[...].astype(jnp.float32), axis=0).astype(jnp.bfloat16)
    for d in range(out_ref.shape[0]):
        out_ref[d] = total


def spread_sum(pieces, copies):
    vmem = pl.BlockSpec(memory_space=pltpu.VMEM)
    return pl.pallas_call(
        spread_kernel,
        in_specs=[vmem],
        out_specs=vmem,
        out_shape=jax.ShapeDtypeStruct((copies,) + pieces.shape[1:], jnp.bfloat16),
        compiler_params=pltpu.CompilerParams(vmem_limit_bytes=16 * 1024 * 1024),
    )(pieces)


def product_kernel(transposed, z_ref, after_ref, *refs):
    *piece_refs, w_ref, out_ref = refs
    depth = piece_refs[0].shape[1]

    def times(piece, k):
        at = pl.multiple_of(lax.rem(z_ref[0] + k + N_Z, N_Z) * depth, depth)
        if transposed:
            w = w_ref[:, pl.ds(at, depth)]
        else:
            w = w_ref[pl.ds(at, depth), :]
        return lax.dot_general(
            piece[...],
            w,
            (((1,), (1 if transposed else 0,)), ((), ())),
            preferred_element_type=jnp.float32,
        )

    total = jnp.concatenate(
        [times(piece_refs[-2], N_Z // 2), times(piece_refs[-1], N_Z // 2)], axis=0
    )
    for piece, k in zip(piece_refs[:-2], DISTANCES, strict=True):
        total = total + times(piece, k)
    out_ref[...] = total.astype(out_ref.dtype)


def product(pieces, weight, transposed, dtype, after):
    rows = pieces[0].shape[0]
    columns = weight.shape[0] if transposed else weight.shape[1]
    z_me = lax.axis_index("z").reshape(1)
    return pl.pallas_call(
        functools.partial(product_kernel, transposed),
        in_specs=[pl.BlockSpec(memory_space=pltpu.SMEM), pl.BlockSpec(memory_space=pl.ANY)]
        + [pl.BlockSpec(memory_space=pltpu.VMEM)] * (len(pieces) + 1),
        out_specs=pl.BlockSpec(memory_space=pltpu.VMEM),
        out_shape=jax.ShapeDtypeStruct((rows, columns), dtype),
        compiler_params=pltpu.CompilerParams(vmem_limit_bytes=24 * 1024 * 1024),
    )(z_me, after, *pieces, weight)


def shards(activations, w_query, w_keyval, w_out, targets, segments):
    block = lax.axis_index(DP)
    tail_docs = lax.dynamic_slice_in_dim(targets, block * MOVE, MOVE) // RECV
    labels = jnp.concatenate([segments[:KEEP], -1 - tail_docs])
    positions, visible = doc_layout(labels)
    cosine, sine = rotation_tables(positions)

    own = lax.all_gather(activations, "yh", axis=1, tiled=True)
    pieces = [own]
    up, down = own, own
    for _ in range(1, N_Z // 2):
        up = lax.ppermute(up, "z", ring(N_Z, 1))
        down = lax.ppermute(down, "z", ring(N_Z, -1))
        pieces += [up, down]
    half = SEQ // 2
    pieces.append(lax.ppermute(up[:half], "z", ring(N_Z, 1)))
    pieces.append(lax.ppermute(down[half:], "z", ring(N_Z, -1)))
    keyval = product(pieces, w_keyval.T, True, jnp.bfloat16, lax.axis_index("z").reshape(1))
    key, value, whole = move_keyval(keyval)
    query = product(pieces, w_query, False, jnp.float32, whole)

    query_rot = rotate(query.reshape(SEQ, 2, HD), cosine, sine).astype(jnp.bfloat16)
    key_rot = rotate(key.astype(jnp.float32), cosine, sine).astype(jnp.bfloat16)
    attended = attend(query_rot.reshape(SEQ, 1, 2, HD), key_rot, value, visible)

    kept, moving = output_partials(attended, w_out)
    kept = lax.psum_scatter(kept.T, "z", scatter_dimension=0, tiled=True).T
    moving = lax.all_to_all(moving, TENSOR, 0, 0, tiled=True)
    moving = spread_sum(moving, targets.shape[0] // MOVE)
    tails = lax.all_to_all(moving, DP, 0, 0, tiled=True)
    kept = kept.reshape(KEEP, N_Y, -1).transpose(1, 0, 2)
    kept = sum_pieces(lax.all_to_all(kept, "yh", 0, 0, tiled=True))

    slots = lax.iota(jnp.int32, RECV)
    wanted = targets - block * RECV
    select = (slots[:, None] == wanted[None, :]).astype(jnp.bfloat16)
    tails = tails.reshape(targets.shape[0], -1)
    arrived = jnp.dot(select, tails, preferred_element_type=jnp.float32).astype(jnp.bfloat16)
    return jnp.concatenate([kept, arrived], axis=0)


def solution(mesh):
    fine = Mesh(
        mesh.devices.reshape(8, 2, 2, N_Z, N_Y), ("x", "yl", "core", "z", "yh")
    )
    placed = (
        P(DP, TENSOR),
        P(None, TENSOR),
        P(None, TENSOR),
        P(TENSOR, None),
        P(),
        P(DP),
    )
    return jax.shard_map(
        shards, mesh=fine, in_specs=placed, out_specs=P(DP, TENSOR), check_vma=False
    )
```

```python
import functools
import math

import jax
import jax.numpy as jnp
from jax import lax
from jax.experimental import pallas as pl
from jax.experimental.pallas import tpu as pltpu
from jax.sharding import Mesh
from jax.sharding import PartitionSpec as P

HQ = 64
KVH = 8
HD = 128
KEEP = 96
MOVE = 32
RECV = 64
SEQ = 128

N_Z = 8
N_Y = 4
DISTANCES = (0, -1, 1, -2, 2, -3, 3)
DP = ("x", "yl", "core")
TENSOR = ("z", "yh")

rope_base = 500000.0


def rotation_tables(positions):
    half = HD // 2
    freqs = rope_base ** (-(jnp.arange(half, dtype=jnp.float32) * 2.0 / HD))
    angles = positions.astype(jnp.float32)[:, None] * freqs[None, :]
    return (jnp.cos(angles), jnp.sin(angles))


def rotate(values, cosine, sine):
    half = HD // 2
    first = values[..., :half]
    second = values[..., half:]
    cosine = cosine[:, None, :]
    sine = sine[:, None, :]
    return jnp.concatenate(
        [first * cosine - second * sine, second * cosine + first * sine], axis=-1
    )


def doc_layout(segment):
    same = segment[:, None] == segment[None, :]
    indices = jnp.arange(segment.shape[0])
    earlier = indices[None, :] < indices[:, None]
    positions = jnp.sum(jnp.logical_and(same, earlier), axis=1)
    visible = jnp.logical_and(same, indices[None, :] <= indices[:, None])
    return (positions, visible)


def attend(query_rot, key_rot, value_rows, visible):
    count = query_rot.shape[0]
    scores = jnp.einsum(
        "rkgd,ckd->kgrc", query_rot, key_rot, preferred_element_type=jnp.float32
    ) / math.sqrt(HD)
    scores = jnp.where(visible[None, None], scores, -1e30)
    top = jnp.max(scores, axis=-1, keepdims=True)
    expd = jnp.exp(scores - top)
    weights = (expd / jnp.sum(expd, axis=-1, keepdims=True)).astype(jnp.bfloat16)
    result = jnp.einsum("kgrc,ckd->rkgd", weights, value_rows, preferred_element_type=jnp.float32)
    return result.astype(jnp.bfloat16).reshape(count, -1)


def ring(n, k):
    return [(i, (i + k) % n) for i in range(n)]


def move_keyval(keyval):
    rows = keyval.shape[0]
    y_me = lax.axis_index("yh")
    other = lax.ppermute(keyval, "yh", [(i, i ^ 1) for i in range(N_Y)])
    low = y_me % 2 == 0
    whole = jnp.concatenate(
        [jnp.where(low, keyval, other), jnp.where(low, other, keyval)], axis=1
    )
    half = N_Z * N_Y // 2

    def routes(flip):
        return [
            (s, N_Y * ((s % half) // 2) + s % 2 + 2 * ((s // half) ^ flip)) for s in range(2 * half)
        ]

    straight = lax.ppermute(whole, TENSOR, routes(0))
    crossed = lax.ppermute(whole, TENSOR, routes(1))
    first = y_me < 2
    key = jnp.where(first, straight, crossed)
    value = jnp.where(first, crossed, straight)
    return key.reshape(rows, 1, HD), value.reshape(rows, 1, HD), whole


def sum_pieces(pieces):
    return jnp.sum(pieces.astype(jnp.float32), axis=0).astype(jnp.bfloat16)


def output_kernel(attended_ref, w_ref, kept_ref, tail_ref, held, rows_held, sems, out_sems):
    wide = held.shape[2]
    width = tail_ref.shape[2]
    copies = [
        pltpu.make_async_copy(w_ref.at[:, pl.ds(z * wide, wide)], held.at[z], sems.at[z])
        for z in range(N_Z)
    ]
    outs = [
        pltpu.make_async_copy(
            rows_held.at[z], kept_ref.at[:, pl.ds(z * wide, wide)], out_sems.at[z]
        )
        for z in range(N_Z)
    ]
    for copy in copies:
        copy.start()
    for z in range(N_Z):
        copies[z].wait()
        rows = jnp.dot(attended_ref[...], held[z], preferred_element_type=jnp.float32)
        rows = rows.astype(jnp.bfloat16)
        rows_held[z] = rows[:KEEP]
        outs[z].start()
        for y in range(N_Y):
            tail_ref[z * N_Y + y] = rows[KEEP:, y * width : (y + 1) * width]
    for copy in outs:
        copy.wait()


def output_partials(attended, w_out):
    depth, columns = w_out.shape
    wide = columns // N_Z
    n = N_Z * N_Y
    vmem, anywhere = pl.BlockSpec(memory_space=pltpu.VMEM), pl.BlockSpec(memory_space=pl.ANY)
    return pl.pallas_call(
        output_kernel,
        in_specs=[vmem, anywhere],
        out_specs=[pl.BlockSpec(memory_space=pltpu.HBM), vmem],
        out_shape=[
            jax.ShapeDtypeStruct((KEEP, columns), jnp.bfloat16),
            jax.ShapeDtypeStruct((n, MOVE, columns // n), jnp.bfloat16),
        ],
        scratch_shapes=[
            pltpu.VMEM((N_Z, depth, wide), jnp.bfloat16),
            pltpu.VMEM((N_Z, KEEP, wide), jnp.bfloat16),
            pltpu.SemaphoreType.DMA((N_Z,)),
            pltpu.SemaphoreType.DMA((N_Z,)),
        ],
        compiler_params=pltpu.CompilerParams(vmem_limit_bytes=32 * 1024 * 1024),
    )(attended, pltpu.with_memory_space_constraint(w_out, pltpu.HBM))


def spread_kernel(pieces_ref, out_ref):
    total = jnp.sum(pieces_ref[...].astype(jnp.float32), axis=0).astype(jnp.bfloat16)
    for d in range(out_ref.shape[0]):
        out_ref[d] = total


def spread_sum(pieces, copies):
    vmem = pl.BlockSpec(memory_space=pltpu.VMEM)
    return pl.pallas_call(
        spread_kernel,
        in_specs=[vmem],
        out_specs=vmem,
        out_shape=jax.ShapeDtypeStruct((copies,) + pieces.shape[1:], jnp.bfloat16),
        compiler_params=pltpu.CompilerParams(vmem_limit_bytes=16 * 1024 * 1024),
    )(pieces)


def product_kernel(transposed, z_ref, after_ref, *refs):
    *piece_refs, w_ref, out_ref = refs
    depth = piece_refs[0].shape[1]

    def times(piece, k):
        at = pl.multiple_of(lax.rem(z_ref[0] + k + N_Z, N_Z) * depth, depth)
        if transposed:
            w = w_ref[:, pl.ds(at, depth)]
        else:
            w = w_ref[pl.ds(at, depth), :]
        return lax.dot_general(
            piece[...],
            w,
            (((1,), (1 if transposed else 0,)), ((), ())),
            preferred_element_type=jnp.float32,
        )

    total = jnp.concatenate(
        [times(piece_refs[-2], N_Z // 2), times(piece_refs[-1], N_Z // 2)], axis=0
    )
    for piece, k in zip(piece_refs[:-2], DISTANCES, strict=True):
        total = total + times(piece, k)
    out_ref[...] = total.astype(out_ref.dtype)


def product(pieces, weight, transposed, dtype, after):
    rows = pieces[0].shape[0]
    columns = weight.shape[0] if transposed else weight.shape[1]
    z_me = lax.axis_index("z").reshape(1)
    return pl.pallas_call(
        functools.partial(product_kernel, transposed),
        in_specs=[pl.BlockSpec(memory_space=pltpu.SMEM), pl.BlockSpec(memory_space=pl.ANY)]
        + [pl.BlockSpec(memory_space=pltpu.VMEM)] * (len(pieces) + 1),
        out_specs=pl.BlockSpec(memory_space=pltpu.VMEM),
        out_shape=jax.ShapeDtypeStruct((rows, columns), dtype),
        compiler_params=pltpu.CompilerParams(vmem_limit_bytes=24 * 1024 * 1024),
    )(z_me, after, *pieces, weight)


def early_kernel(z_ref, *refs):
    *piece_refs, w_ref, out_ref, last_ref = refs
    depth = piece_refs[0].shape[1]

    def columns(k):
        at = pl.multiple_of(lax.rem(z_ref[0] + k + N_Z, N_Z) * depth, depth)
        return w_ref[:, pl.ds(at, depth)]

    total = jnp.zeros(out_ref.shape, jnp.float32)
    for piece, k in zip(piece_refs, DISTANCES, strict=True):
        total = total + lax.dot_general(
            piece[...], columns(k), (((1,), (1,)), ((), ())), preferred_element_type=jnp.float32
        )
    out_ref[...] = total
    last_ref[...] = columns(N_Z // 2)


def late_kernel(total_ref, up_ref, down_ref, w_ref, out_ref):
    half = up_ref.shape[0]
    for at, piece in ((0, up_ref), (half, down_ref)):
        rows = lax.dot_general(
            piece[...], w_ref[...], (((1,), (1,)), ((), ())), preferred_element_type=jnp.float32
        )
        out_ref[at : at + half] = (total_ref[at : at + half] + rows).astype(jnp.bfloat16)


def keyval_product(pieces, weight):
    rows, depth = pieces[0].shape
    columns = weight.shape[0]
    vmem = pl.BlockSpec(memory_space=pltpu.VMEM)
    params = pltpu.CompilerParams(vmem_limit_bytes=16 * 1024 * 1024)
    total, last = pl.pallas_call(
        early_kernel,
        in_specs=[pl.BlockSpec(memory_space=pltpu.SMEM)] + [vmem] * (len(pieces) - 1),
        out_specs=[vmem] * 2,
        out_shape=[
            jax.ShapeDtypeStruct((rows, columns), jnp.float32),
            jax.ShapeDtypeStruct((columns, depth), jnp.bfloat16),
        ],
        compiler_params=params,
    )(lax.axis_index("z").reshape(1), *pieces[:-2], weight)
    return pl.pallas_call(
        late_kernel,
        in_specs=[vmem] * 4,
        out_specs=vmem,
        out_shape=jax.ShapeDtypeStruct((rows, columns), jnp.bfloat16),
        compiler_params=params,
    )(total, *pieces[-2:], last)


def shards(activations, w_query, w_keyval, w_out, targets, segments):
    block = lax.axis_index(DP)
    tail_docs = lax.dynamic_slice_in_dim(targets, block * MOVE, MOVE) // RECV
    labels = jnp.concatenate([segments[:KEEP], -1 - tail_docs])
    positions, visible = doc_layout(labels)
    cosine, sine = rotation_tables(positions)

    own = lax.all_gather(activations, "yh", axis=1, tiled=True)
    pieces = [own]
    up, down = own, own
    for _ in range(1, N_Z // 2):
        up = lax.ppermute(up, "z", ring(N_Z, 1))
        down = lax.ppermute(down, "z", ring(N_Z, -1))
        pieces += [up, down]
    half = SEQ // 2
    pieces.append(lax.ppermute(up[:half], "z", ring(N_Z, 1)))
    pieces.append(lax.ppermute(down[half:], "z", ring(N_Z, -1)))
    keyval = keyval_product(pieces, w_keyval.T)
    key, value, whole = move_keyval(keyval)
    query = product(pieces, w_query, False, jnp.float32, whole)

    query_rot = rotate(query.reshape(SEQ, 2, HD), cosine, sine).astype(jnp.bfloat16)
    key_rot = rotate(key.astype(jnp.float32), cosine, sine).astype(jnp.bfloat16)
    attended = attend(query_rot.reshape(SEQ, 1, 2, HD), key_rot, value, visible)

    kept, moving = output_partials(attended, w_out)
    kept = lax.psum_scatter(kept.T, "z", scatter_dimension=0, tiled=True).T
    moving = lax.all_to_all(moving, TENSOR, 0, 0, tiled=True)
    moving = spread_sum(moving, targets.shape[0] // MOVE)
    tails = lax.all_to_all(moving, DP, 0, 0, tiled=True)
    kept = kept.reshape(KEEP, N_Y, -1).transpose(1, 0, 2)
    kept = sum_pieces(lax.all_to_all(kept, "yh", 0, 0, tiled=True))

    slots = lax.iota(jnp.int32, RECV)
    wanted = targets - block * RECV
    select = (slots[:, None] == wanted[None, :]).astype(jnp.bfloat16)
    tails = tails.reshape(targets.shape[0], -1)
    arrived = jnp.dot(select, tails, preferred_element_type=jnp.float32).astype(jnp.bfloat16)
    return jnp.concatenate([kept, arrived], axis=0)


def solution(mesh):
    fine = Mesh(
        mesh.devices.reshape(8, 2, 2, N_Z, N_Y), ("x", "yl", "core", "z", "yh")
    )
    placed = (
        P(DP, TENSOR),
        P(None, TENSOR),
        P(None, TENSOR),
        P(TENSOR, None),
        P(),
        P(DP),
    )
    return jax.shard_map(
        shards, mesh=fine, in_specs=placed, out_specs=P(DP, TENSOR), check_vma=False
    )
```

```python
import functools
import math

import jax
import jax.numpy as jnp
from jax import lax
from jax.experimental import pallas as pl
from jax.experimental.pallas import tpu as pltpu
from jax.sharding import Mesh
from jax.sharding import PartitionSpec as P

HQ = 64
KVH = 8
HD = 128
KEEP = 96
MOVE = 32
RECV = 64
SEQ = 128

N_Z = 8
N_Y = 4
DISTANCES = (0, -1, 1, -2, 2, -3, 3)
DP = ("x", "yl", "core")
TENSOR = ("z", "yh")

rope_base = 500000.0


def rotation_tables(positions):
    half = HD // 2
    freqs = rope_base ** (-(jnp.arange(half, dtype=jnp.float32) * 2.0 / HD))
    angles = positions.astype(jnp.float32)[:, None] * freqs[None, :]
    return (jnp.cos(angles), jnp.sin(angles))


def rotate(values, cosine, sine):
    half = HD // 2
    first = values[..., :half]
    second = values[..., half:]
    cosine = cosine[:, None, :]
    sine = sine[:, None, :]
    return jnp.concatenate(
        [first * cosine - second * sine, second * cosine + first * sine], axis=-1
    )


def doc_layout(segment):
    same = segment[:, None] == segment[None, :]
    indices = jnp.arange(segment.shape[0])
    earlier = indices[None, :] < indices[:, None]
    positions = jnp.sum(jnp.logical_and(same, earlier), axis=1)
    visible = jnp.logical_and(same, indices[None, :] <= indices[:, None])
    return (positions, visible)


def attend(query_rot, key_rot, value_rows, visible):
    count = query_rot.shape[0]
    scores = jnp.einsum(
        "rkgd,ckd->kgrc", query_rot, key_rot, preferred_element_type=jnp.float32
    ) / math.sqrt(HD)
    scores = jnp.where(visible[None, None], scores, -1e30)
    top = jnp.max(scores, axis=-1, keepdims=True)
    expd = jnp.exp(scores - top)
    weights = (expd / jnp.sum(expd, axis=-1, keepdims=True)).astype(jnp.bfloat16)
    result = jnp.einsum("kgrc,ckd->rkgd", weights, value_rows, preferred_element_type=jnp.float32)
    return result.astype(jnp.bfloat16).reshape(count, -1)


def ring(n, k):
    return [(i, (i + k) % n) for i in range(n)]


def keyval_routes(k):
    half = N_Z * N_Y // 2
    return [
        (s, N_Y * ((s % half) // 2) + (s % 2 + 2 * (s // half) + k) % N_Y) for s in range(2 * half)
    ]


def move_keyval(keyval):
    rows = keyval.shape[0]
    y_me = lax.axis_index("yh")
    pieces = [lax.ppermute(keyval, TENSOR, keyval_routes(k)) for k in range(N_Y)]
    stack = jnp.stack(pieces)
    roles = [lax.dynamic_index_in_dim(stack, (y_me - r) % N_Y, 0, False) for r in range(N_Y)]
    key = jnp.concatenate(roles[:2], axis=1).reshape(rows, 1, HD)
    value = jnp.concatenate(roles[2:], axis=1).reshape(rows, 1, HD)
    return key, value


def sum_pieces(pieces):
    return jnp.sum(pieces.astype(jnp.float32), axis=0).astype(jnp.bfloat16)


def output_kernel(attended_ref, w_ref, kept_ref, tail_ref, held, rows_held, sems, out_sems):
    wide = held.shape[2]
    width = tail_ref.shape[2]
    copies = [
        pltpu.make_async_copy(w_ref.at[:, pl.ds(z * wide, wide)], held.at[z], sems.at[z])
        for z in range(N_Z)
    ]
    outs = [
        pltpu.make_async_copy(
            rows_held.at[z], kept_ref.at[:, pl.ds(z * wide, wide)], out_sems.at[z]
        )
        for z in range(N_Z)
    ]
    for copy in copies:
        copy.start()
    for z in range(N_Z):
        copies[z].wait()
        rows = jnp.dot(attended_ref[...], held[z], preferred_element_type=jnp.float32)
        rows = rows.astype(jnp.bfloat16)
        rows_held[z] = rows[:KEEP]
        outs[z].start()
        for y in range(N_Y):
            tail_ref[z * N_Y + y] = rows[KEEP:, y * width : (y + 1) * width]
    for copy in outs:
        copy.wait()


def output_partials(attended, w_out):
    depth, columns = w_out.shape
    wide = columns // N_Z
    n = N_Z * N_Y
    vmem, anywhere = pl.BlockSpec(memory_space=pltpu.VMEM), pl.BlockSpec(memory_space=pl.ANY)
    return pl.pallas_call(
        output_kernel,
        in_specs=[vmem, anywhere],
        out_specs=[pl.BlockSpec(memory_space=pltpu.HBM), vmem],
        out_shape=[
            jax.ShapeDtypeStruct((KEEP, columns), jnp.bfloat16),
            jax.ShapeDtypeStruct((n, MOVE, columns // n), jnp.bfloat16),
        ],
        scratch_shapes=[
            pltpu.VMEM((N_Z, depth, wide), jnp.bfloat16),
            pltpu.VMEM((N_Z, KEEP, wide), jnp.bfloat16),
            pltpu.SemaphoreType.DMA((N_Z,)),
            pltpu.SemaphoreType.DMA((N_Z,)),
        ],
        compiler_params=pltpu.CompilerParams(vmem_limit_bytes=32 * 1024 * 1024),
    )(attended, pltpu.with_memory_space_constraint(w_out, pltpu.HBM))


def spread_kernel(pieces_ref, out_ref):
    total = jnp.sum(pieces_ref[...].astype(jnp.float32), axis=0).astype(jnp.bfloat16)
    for d in range(out_ref.shape[0]):
        out_ref[d] = total


def spread_sum(pieces, copies):
    vmem = pl.BlockSpec(memory_space=pltpu.VMEM)
    return pl.pallas_call(
        spread_kernel,
        in_specs=[vmem],
        out_specs=vmem,
        out_shape=jax.ShapeDtypeStruct((copies,) + pieces.shape[1:], jnp.bfloat16),
        compiler_params=pltpu.CompilerParams(vmem_limit_bytes=16 * 1024 * 1024),
    )(pieces)


def product_kernel(transposed, z_ref, after_ref, *refs):
    *piece_refs, w_ref, out_ref = refs
    depth = piece_refs[0].shape[1]

    def times(piece, k):
        at = pl.multiple_of(lax.rem(z_ref[0] + k + N_Z, N_Z) * depth, depth)
        if transposed:
            w = w_ref[:, pl.ds(at, depth)]
        else:
            w = w_ref[pl.ds(at, depth), :]
        return lax.dot_general(
            piece[...],
            w,
            (((1,), (1 if transposed else 0,)), ((), ())),
            preferred_element_type=jnp.float32,
        )

    total = jnp.concatenate(
        [times(piece_refs[-2], N_Z // 2), times(piece_refs[-1], N_Z // 2)], axis=0
    )
    for piece, k in zip(piece_refs[:-2], DISTANCES, strict=True):
        total = total + times(piece, k)
    out_ref[...] = total.astype(out_ref.dtype)


def product(pieces, weight, transposed, dtype, after):
    rows = pieces[0].shape[0]
    columns = weight.shape[0] if transposed else weight.shape[1]
    z_me = lax.axis_index("z").reshape(1)
    return pl.pallas_call(
        functools.partial(product_kernel, transposed),
        in_specs=[pl.BlockSpec(memory_space=pltpu.SMEM), pl.BlockSpec(memory_space=pl.ANY)]
        + [pl.BlockSpec(memory_space=pltpu.VMEM)] * (len(pieces) + 1),
        out_specs=pl.BlockSpec(memory_space=pltpu.VMEM),
        out_shape=jax.ShapeDtypeStruct((rows, columns), dtype),
        compiler_params=pltpu.CompilerParams(vmem_limit_bytes=24 * 1024 * 1024),
    )(z_me, after, *pieces, weight)


def early_kernel(z_ref, *refs):
    *piece_refs, w_ref, out_ref, last_ref = refs
    depth = piece_refs[0].shape[1]

    def columns(k):
        at = pl.multiple_of(lax.rem(z_ref[0] + k + N_Z, N_Z) * depth, depth)
        return w_ref[:, pl.ds(at, depth)]

    total = jnp.zeros(out_ref.shape, jnp.float32)
    for piece, k in zip(piece_refs, DISTANCES, strict=True):
        total = total + lax.dot_general(
            piece[...], columns(k), (((1,), (1,)), ((), ())), preferred_element_type=jnp.float32
        )
    out_ref[...] = total
    last_ref[...] = columns(N_Z // 2)


def late_kernel(total_ref, up_ref, down_ref, w_ref, out_ref):
    half = up_ref.shape[0]
    for at, piece in ((0, up_ref), (half, down_ref)):
        rows = lax.dot_general(
            piece[...], w_ref[...], (((1,), (1,)), ((), ())), preferred_element_type=jnp.float32
        )
        out_ref[at : at + half] = (total_ref[at : at + half] + rows).astype(jnp.bfloat16)


def keyval_product(pieces, weight):
    rows, depth = pieces[0].shape
    columns = weight.shape[0]
    vmem = pl.BlockSpec(memory_space=pltpu.VMEM)
    params = pltpu.CompilerParams(vmem_limit_bytes=16 * 1024 * 1024)
    total, last = pl.pallas_call(
        early_kernel,
        in_specs=[pl.BlockSpec(memory_space=pltpu.SMEM)] + [vmem] * (len(pieces) - 1),
        out_specs=[vmem] * 2,
        out_shape=[
            jax.ShapeDtypeStruct((rows, columns), jnp.float32),
            jax.ShapeDtypeStruct((columns, depth), jnp.bfloat16),
        ],
        compiler_params=params,
    )(lax.axis_index("z").reshape(1), *pieces[:-2], weight)
    return pl.pallas_call(
        late_kernel,
        in_specs=[vmem] * 4,
        out_specs=vmem,
        out_shape=jax.ShapeDtypeStruct((rows, columns), jnp.bfloat16),
        compiler_params=params,
    )(total, *pieces[-2:], last)


def shards(activations, w_query, w_keyval, w_out, targets, segments):
    block = lax.axis_index(DP)
    tail_docs = lax.dynamic_slice_in_dim(targets, block * MOVE, MOVE) // RECV
    labels = jnp.concatenate([segments[:KEEP], -1 - tail_docs])
    positions, visible = doc_layout(labels)
    cosine, sine = rotation_tables(positions)

    own = lax.all_gather(activations, "yh", axis=1, tiled=True)
    pieces = [own]
    up, down = own, own
    for _ in range(1, N_Z // 2):
        up = lax.ppermute(up, "z", ring(N_Z, 1))
        down = lax.ppermute(down, "z", ring(N_Z, -1))
        pieces += [up, down]
    half = SEQ // 2
    pieces.append(lax.ppermute(up[:half], "z", ring(N_Z, 1)))
    pieces.append(lax.ppermute(down[half:], "z", ring(N_Z, -1)))
    keyval = keyval_product(pieces, w_keyval.T)
    key, value = move_keyval(keyval)
    query = product(pieces, w_query, False, jnp.float32, keyval)

    query_rot = rotate(query.reshape(SEQ, 2, HD), cosine, sine).astype(jnp.bfloat16)
    key_rot = rotate(key.astype(jnp.float32), cosine, sine).astype(jnp.bfloat16)
    attended = attend(query_rot.reshape(SEQ, 1, 2, HD), key_rot, value, visible)

    kept, moving = output_partials(attended, w_out)
    kept = lax.psum_scatter(kept.T, "z", scatter_dimension=0, tiled=True).T
    moving = lax.all_to_all(moving, TENSOR, 0, 0, tiled=True)
    moving = spread_sum(moving, targets.shape[0] // MOVE)
    tails = lax.all_to_all(moving, DP, 0, 0, tiled=True)
    kept = kept.reshape(KEEP, N_Y, -1).transpose(1, 0, 2)
    kept = sum_pieces(lax.all_to_all(kept, "yh", 0, 0, tiled=True))

    slots = lax.iota(jnp.int32, RECV)
    wanted = targets - block * RECV
    select = (slots[:, None] == wanted[None, :]).astype(jnp.bfloat16)
    tails = tails.reshape(targets.shape[0], -1)
    arrived = jnp.dot(select, tails, preferred_element_type=jnp.float32).astype(jnp.bfloat16)
    return jnp.concatenate([kept, arrived], axis=0)


def solution(mesh):
    fine = Mesh(
        mesh.devices.reshape(8, 2, 2, N_Z, N_Y), ("x", "yl", "core", "z", "yh")
    )
    placed = (
        P(DP, TENSOR),
        P(None, TENSOR),
        P(None, TENSOR),
        P(TENSOR, None),
        P(),
        P(DP),
    )
    return jax.shard_map(
        shards, mesh=fine, in_specs=placed, out_specs=P(DP, TENSOR), check_vma=False
    )
```
